512 devices in a mesh: seq: 16 (over z), tp: 8 (over y, core), dp: 4 (over x).
Axes of the slice: x: 4, y: 4, z: 16, core: 2. Of those that a mesh axis runs over, the one named last changes fastest.
Arguments:
- x_in: bfloat16 [4, 2048, 4096], P('dp', 'seq', 'tp'), may hold values from -7 to 7
- dt_in: bfloat16 [4, 2048, 4096], P('dp', 'seq', 'tp'), may hold values from -2 to 9
- b_in: bfloat16 [4, 16, 2048], P('dp', None, 'seq'), may hold values from -1 to 3
- c_in: bfloat16 [4, 16, 2048], P('dp', None, 'seq'), may hold values from -4 to 4
- dy_in: bfloat16 [4, 2048, 4096], P('dp', 'seq', 'tp'), may hold values from -6 to 6
- a_log: float32 [16, 4096], P(None, 'tp'), may hold values from 0 to 2.77
- d_skip: float32 [4096], P('tp'), may hold values from 0.1 to 1.9
- dt_bias: float32 [4096], P('tp'), may hold values from -14 to -2
- q_in: bfloat16 [4, 2048, 4096], P('dp', 'seq', 'tp'), may hold values from -8 to 8
- k_in: bfloat16 [4, 2048, 1024], P('dp', 'seq', 'tp'), may hold values from -6 to 6
- value_input: bfloat16 [4, 2048, 1024], P('dp', 'seq', 'tp'), may hold values from -6 to 6
- dout_in: bfloat16 [4, 2048, 4096], P('dp', 'seq', 'tp'), may hold values from -6 to 6
- doc_lengths: int32 [4, 8], P('dp'), may hold values from 1 to 1600, 2048 in all within a row
- plan: int32 [4, 64], P('dp'), may hold values from 0 to 63, each once within a row
Outputs:
- ssm_out: bfloat16 [4, 2048, 4096], P('dp', 'seq', 'tp')
- x_grad: bfloat16 [4, 2048, 4096], P('dp', 'seq', 'tp')
- dt_grad: bfloat16 [4, 2048, 4096], P('dp', 'seq', 'tp')
- b_grad: float32 [4, 16, 2048], P('dp', None, 'seq')
- c_grad: float32 [4, 16, 2048], P('dp', None, 'seq')
- a_log_grad: float32 [16, 4096], P(None, 'tp')
- d_skip_grad: float32 [4096], P('tp')
- dt_bias_grad: float32 [4096], P('tp')
- attn_out: bfloat16 [4, 2048, 4096], P('dp', 'seq', 'tp')
- query_gradient: bfloat16 [4, 2048, 4096], P('dp', 'seq', 'tp')
- key_gradient: bfloat16 [4, 2048, 1024], P('dp', 'seq', 'tp')
- value_gradient: bfloat16 [4, 2048, 1024], P('dp', 'seq', 'tp')
The draws below stay inside these ranges and needn't reach their ends.
All inputs are finite; a program needn't handle non-finite values.
Results may differ from the reference program's by a relative error of at most 0.04.
Values may be sent and summed in bfloat16 or wider, within the bound.
No kernel may reach another device: no remote copies, remote signals or barrier semaphores. Data moves between devices by JAX's collectives and lax.ppermute only.
A program may use at most 64 MiB of HBM per device.

```python
import math
import jax
import jax.numpy as jnp
import numpy as np
from jax import lax

DI = 4096
NS = 16
QUERY_HEADS = 32
KEY_VALUE_HEADS = 8
HEAD_SIZE = 128
BLOCK = 32
DOCS = 8
SEQUENCE_LENGTH = 2048
SEQUENCE_COUNT = 4
BLOCKS = 64
LONGEST = 1600


def draw_q_in(key, part):
    key = jax.random.fold_in(key, 11)
    value_tensor = jnp.clip(jax.random.normal(key, (SEQUENCE_COUNT, SEQUENCE_LENGTH, KEY_VALUE_HEADS, QUERY_HEADS // KEY_VALUE_HEADS, HEAD_SIZE)), -6.0, 6.0)
    return value_tensor.reshape(SEQUENCE_COUNT, SEQUENCE_LENGTH, QUERY_HEADS * HEAD_SIZE).astype(jnp.bfloat16)


def draw_k_in(key, part):
    key = jax.random.fold_in(key, 12)
    value_tensor = jnp.clip(jax.random.normal(key, (SEQUENCE_COUNT, SEQUENCE_LENGTH, KEY_VALUE_HEADS, HEAD_SIZE)), -6.0, 6.0)
    return value_tensor.reshape(SEQUENCE_COUNT, SEQUENCE_LENGTH, KEY_VALUE_HEADS * HEAD_SIZE).astype(jnp.bfloat16)


def draw_dt_in(key, part):
    key = jax.random.fold_in(key, 21)
    noise_key, assignment_seed = jax.random.split(key)
    spike_clusters = jax.random.randint(assignment_seed, (SEQUENCE_COUNT, 1, 6), 0, SEQUENCE_LENGTH)
    assignment_table = jnp.arange(SEQUENCE_LENGTH, dtype=jnp.int32)[None, :, None]
    spike_cluster = jnp.any(assignment_table == spike_clusters, axis=2).astype(jnp.float32)[:, :, None]
    jitter_sample = 0.5 * jnp.clip(jax.random.normal(noise_key, (SEQUENCE_COUNT, SEQUENCE_LENGTH, DI)), -4.0, 4.0)
    return (jitter_sample + 7.0 * spike_cluster).astype(jnp.bfloat16)


def draw_dt_bias(key, part):
    key = jax.random.fold_in(key, 22)
    pick_key, rate_key = jax.random.split(key)
    share = 0.5
    slow = jax.random.uniform(pick_key, (DI,)) < share
    unit = jax.random.uniform(rate_key, (DI,))
    slow_rate = 0.05 / SEQUENCE_LENGTH * 3.0 ** unit
    fast_rate = 0.025 * 2.4 ** unit
    rate = jnp.where(slow, slow_rate, fast_rate)
    return jnp.log(jnp.expm1(rate))


def draw_x_in(key, part):
    key = jax.random.fold_in(key, 31)
    centre_key, noise_key = jax.random.split(key)
    centre = jax.random.uniform(centre_key, (1, 1, DI), minval=-1.0, maxval=1.0)
    jitter_sample = jnp.clip(jax.random.normal(noise_key, (SEQUENCE_COUNT, SEQUENCE_LENGTH, DI)), -5.0, 5.0)
    return (centre + jitter_sample).astype(jnp.bfloat16)


def draw_b_in(key, part):
    key = jax.random.fold_in(key, 41)
    value_tensor = 1.0 + 0.5 * jnp.clip(jax.random.normal(key, (SEQUENCE_COUNT, NS, SEQUENCE_LENGTH)), -4.0, 4.0)
    return value_tensor.astype(jnp.bfloat16)


def steps_of(stream_key, shape, shards, smallest, high):
    def one(axis_at, blocks):
        steps = jax.random.uniform(jax.random.fold_in(jax.random.fold_in(stream_key, 6), axis_at), (blocks,), jnp.float32, smallest / len(shards), high / len(shards))
        return jnp.repeat(jnp.exp(steps), shape[axis_at] // blocks).reshape((-1,) + (1,) * (len(shape) - axis_at - 1))

    gain = one(*shards[0])
    for cut in shards[1:]:
        gain = gain * one(*cut)
    return gain


def profile(number_of, total, limit, slope):
    loads = [(1 << 20) // math.isqrt(rank ** slope) + 1 for rank in range(2, number_of + 1)]
    spare, given = total - limit - (number_of - 1), [1] * (number_of - 1)
    while spare > 0:
        movable = [i for i in range(number_of - 1) if given[i] < limit]
        whole, budget = sum([loads[i] for i in movable]), spare
        for i in movable:
            more = min(limit - given[i], max(1, budget * loads[i] // whole), spare)
            given[i] = given[i] + more
            spare = spare - more
    return np.array([limit] + given)


def uneven_parts(rng, amount, total, limit, skew):
    if amount == 2:
        one = jax.random.randint(rng, (), max(1, total - limit), min(limit, total - 1) + 1)
        return jnp.stack([one, total - one])
    sizes = jnp.asarray(profile(amount, total, limit, skew), jnp.int32)
    pairs = (amount - 1) // 2
    giver, receiver = sizes[1:1 + 2 * pairs:2], sizes[2:2 + 2 * pairs:2]
    room = jnp.minimum(giver - 1, limit - receiver)
    passed = jax.random.randint(jax.random.fold_in(rng, 1), (pairs,), 0, 1 << 20) % (room + 1)
    sizes = sizes.at[1:1 + 2 * pairs:2].set(giver - passed).at[2:2 + 2 * pairs:2].set(receiver + passed)
    return sizes[jax.random.permutation(jax.random.fold_in(rng, 2), amount)]


def bell_draw(own_key, dims, deviation, bound, cuts=(), kind=jnp.bfloat16):
    values = jax.random.normal(own_key, dims, jnp.float32) * deviation
    if len(cuts) > 0:
        values = steps_of(own_key, dims, cuts, -0.22, 0.18) * values
    return jnp.clip(values, min=-bound, max=bound).astype(kind)


def setup_inputs(seed: int = 0) -> dict:
    keys = jax.random.split(jax.random.key(seed), 15)
    x_in = draw_x_in(jax.random.fold_in(keys[14], 71), 0)
    dt_in = draw_dt_in(jax.random.fold_in(keys[14], 71), 0)
    b_in = draw_b_in(jax.random.fold_in(keys[14], 71), 0)
    c_in = bell_draw(keys[3], (SEQUENCE_COUNT, NS, SEQUENCE_LENGTH), 0.5, 4.0, ((0, 4), (2, 16)))
    dy_in = bell_draw(keys[4], (SEQUENCE_COUNT, SEQUENCE_LENGTH, DI), 1.0, 6.0, ((0, 4), (1, 16), (2, 8)))
    a_log = jnp.clip(2.77 * jax.random.uniform(keys[5], (NS, DI), jnp.float32) ** steps_of(keys[5], (NS, DI), ((1, 8),), -0.2, 0.2), 0.0, 2.77)
    d_skip = jnp.clip(1.0 + 0.18 * jax.random.normal(keys[6], (DI,), jnp.float32), 0.1, 1.9)
    dt_bias = draw_dt_bias(jax.random.fold_in(keys[14], 71), 0)
    q_in = draw_q_in(jax.random.fold_in(keys[14], 71), 0)
    k_in = draw_k_in(jax.random.fold_in(keys[14], 71), 0)
    value_input = bell_draw(keys[10], (SEQUENCE_COUNT, SEQUENCE_LENGTH, KEY_VALUE_HEADS * HEAD_SIZE), 1.0, 6.0, ((0, 4), (1, 16), (2, 8)))
    dout_in = bell_draw(keys[11], (SEQUENCE_COUNT, SEQUENCE_LENGTH, QUERY_HEADS * HEAD_SIZE), 1.0, 6.0, ((0, 4), (1, 16), (2, 8)))
    doc_lengths = jax.vmap(lambda own: uneven_parts(own, DOCS, SEQUENCE_LENGTH, LONGEST, 2))(jax.random.split(keys[12], SEQUENCE_COUNT)).reshape((SEQUENCE_COUNT, DOCS)).astype(jnp.int32)
    plan = jax.vmap(lambda own: jax.random.permutation(own, BLOCKS))(jax.random.split(keys[13], SEQUENCE_COUNT)).reshape((SEQUENCE_COUNT, BLOCKS)).astype(jnp.int32)
    return dict(x_in=x_in, dt_in=dt_in, b_in=b_in, c_in=c_in, dy_in=dy_in, a_log=a_log, d_skip=d_skip, dt_bias=dt_bias, q_in=q_in, k_in=k_in, value_input=value_input, dout_in=dout_in, doc_lengths=doc_lengths, plan=plan)


def pair_combine(earlier, later):
    return (earlier[0] * later[0], later[0] * earlier[1] + later[1])

def document_tables(lengths):
    ends = jnp.cumsum(lengths)
    starts = ends - lengths
    assignment_table = jnp.arange(SEQUENCE_LENGTH, dtype=jnp.int32)
    doc_of = lax.optimization_barrier(jnp.sum((assignment_table[:, None] >= ends[None, :]).astype(jnp.int32), axis=1))
    first = jnp.any(assignment_table[:, None] == starts[None, :], axis=1)
    return (doc_of, first)

def ssm_block(inputs, raw, b_rows, c_rows, a_block, skip_block, bias_block, keep):
    delta = jax.nn.softplus(raw + bias_block)
    rates = -jnp.exp(a_block)
    decay = jnp.exp(delta[:, None, :] * rates[None]) * keep[:, None, None]
    drive = delta[:, None, :] * b_rows.T[:, :, None] * inputs[:, None, :]
    factors, states = lax.associative_scan(pair_combine, (decay, drive))
    return lax.optimization_barrier(jnp.sum(c_rows.T[:, :, None] * states, axis=1)) + skip_block * inputs

def ssm_row(x_row, dt_row, b_row, c_row, dy_row, lengths, a_log, d_skip, dt_bias):
    doc_of, first = document_tables(lengths)
    keep = 1.0 - first.astype(jnp.float32)
    width = math.gcd(DI, 512)
    count = DI // width

    def to_blocks(value_tensor):
        return jnp.moveaxis(value_tensor.astype(jnp.float32).reshape(SEQUENCE_LENGTH, count, width), 1, 0)
    b_rows = b_row.astype(jnp.float32)
    c_rows = c_row.astype(jnp.float32)

    def one_block(parts):
        inputs, raw, upstream, a_block, skip_block, bias_block = parts

        def forward(inputs, raw, b_rows, c_rows, a_block, skip_block, bias_block):
            return ssm_block(inputs, raw, b_rows, c_rows, a_block, skip_block, bias_block, keep)
        output, pull = jax.vjp(forward, inputs, raw, b_rows, c_rows, a_block, skip_block, bias_block)
        grads = pull(upstream)
        return (output,) + tuple(grads)
    results = lax.map(one_block, (to_blocks(x_row), to_blocks(dt_row), to_blocks(dy_row), jnp.moveaxis(a_log.reshape(NS, count, width), 1, 0), d_skip.reshape(count, width), dt_bias.reshape(count, width)))
    output, x_grad, dt_grad, b_grad, c_grad, a_grad, skip_grad, bias_grad = results

    def to_row(value_tensor):
        return jnp.moveaxis(value_tensor, 0, 1).reshape(SEQUENCE_LENGTH, DI)
    return (to_row(output).astype(jnp.bfloat16), to_row(x_grad).astype(jnp.bfloat16), to_row(dt_grad).astype(jnp.bfloat16), lax.optimization_barrier(jnp.sum(b_grad, axis=0)), lax.optimization_barrier(jnp.sum(c_grad, axis=0)), jnp.moveaxis(a_grad, 0, 1).reshape(NS, DI), skip_grad.reshape(DI), bias_grad.reshape(DI))

def attention_row(query_row_slice, key_row_slice, value_row_slice, dout_row, lengths, planned_row):
    doc_of, first = document_tables(lengths)
    assignment_table = jnp.arange(SEQUENCE_LENGTH, dtype=jnp.int32)
    allowed = (assignment_table[None, :] <= assignment_table[:, None]) & (doc_of[None, :] == doc_of[:, None])
    query_group = QUERY_HEADS // KEY_VALUE_HEADS
    width = QUERY_HEADS * HEAD_SIZE
    scale = HEAD_SIZE ** (-0.5)
    gradient_planned = dout_row.reshape(BLOCKS, BLOCK, width)
    gradient_unplanned = jnp.zeros_like(gradient_planned).at[planned_row].set(gradient_planned).reshape(SEQUENCE_LENGTH, KEY_VALUE_HEADS, query_group, HEAD_SIZE)
    query_tensor = query_row_slice.reshape(SEQUENCE_LENGTH, KEY_VALUE_HEADS, query_group, HEAD_SIZE)
    key_tensor = key_row_slice.reshape(SEQUENCE_LENGTH, KEY_VALUE_HEADS, HEAD_SIZE)
    value_tensor = value_row_slice.reshape(SEQUENCE_LENGTH, KEY_VALUE_HEADS, HEAD_SIZE)

    def head(parts):
        query_rows, key_rows, value_rows, d_rows = parts
        query32 = query_rows.astype(jnp.float32)
        key32 = key_rows.astype(jnp.float32)
        value32 = value_rows.astype(jnp.float32)
        d32 = d_rows.astype(jnp.float32)
        scores = jnp.einsum('qgd,kd->gqk', query32, key32) * scale
        top = lax.optimization_barrier(jnp.max(jnp.where(allowed, scores, -jnp.inf), axis=-1))
        total = lax.optimization_barrier(jnp.sum(jnp.where(allowed, jnp.exp(scores - top[..., None]), 0.0), axis=-1))
        lse = top + jnp.log(total)
        probs = jnp.where(allowed, jnp.exp(scores - lse[..., None]), 0.0)
        probs_half = lax.optimization_barrier(probs.astype(jnp.bfloat16)).astype(jnp.float32)
        attended_output = jnp.einsum('gqk,kd->qgd', probs_half, value32).astype(jnp.bfloat16)
        rowdot = lax.optimization_barrier(jnp.sum(d32 * attended_output.astype(jnp.float32), axis=-1)).T
        d_prob = jnp.einsum('qgd,kd->gqk', d32, value32)
        d_score = lax.optimization_barrier((probs * (d_prob - rowdot[..., None])).astype(jnp.bfloat16)).astype(jnp.float32)
        query_gradient = (jnp.einsum('gqk,kd->qgd', d_score, key32) * scale).astype(jnp.bfloat16)
        key_gradient = (jnp.einsum('gqk,qgd->kd', d_score, query32) * scale).astype(jnp.bfloat16)
        value_gradient = jnp.einsum('gqk,qgd->kd', probs_half, d32).astype(jnp.bfloat16)
        return (attended_output, query_gradient, key_gradient, value_gradient)
    attended_output, query_gradient, key_gradient, value_gradient = lax.map(head, (jnp.moveaxis(query_tensor, 1, 0), jnp.moveaxis(key_tensor, 1, 0), jnp.moveaxis(value_tensor, 1, 0), jnp.moveaxis(gradient_unplanned, 1, 0)))

    def into_plan_order(values_by_head):
        flat = jnp.moveaxis(values_by_head, 0, 1).reshape(BLOCKS, BLOCK, width)
        return flat[planned_row].reshape(SEQUENCE_LENGTH, width)
    return (into_plan_order(attended_output), into_plan_order(query_gradient), jnp.moveaxis(key_gradient, 0, 1).reshape(SEQUENCE_LENGTH, KEY_VALUE_HEADS * HEAD_SIZE), jnp.moveaxis(value_gradient, 0, 1).reshape(SEQUENCE_LENGTH, KEY_VALUE_HEADS * HEAD_SIZE))

def reference(x_in, dt_in, b_in, c_in, dy_in, a_log, d_skip, dt_bias, q_in, k_in, value_input, dout_in, doc_lengths, plan):

    def ssm_map(parts):
        return ssm_row(parts[0], parts[1], parts[2], parts[3], parts[4], parts[5], a_log, d_skip, dt_bias)

    def attention_map(parts):
        return attention_row(parts[0], parts[1], parts[2], parts[3], parts[4], parts[5])
    mixer = lax.map(ssm_map, (x_in, dt_in, b_in, c_in, dy_in, doc_lengths))
    attention = lax.map(attention_map, (q_in, k_in, value_input, dout_in, doc_lengths, plan))
    return (mixer[0], mixer[1], mixer[2], mixer[3], mixer[4], lax.optimization_barrier(jnp.sum(mixer[5], axis=0)), lax.optimization_barrier(jnp.sum(mixer[6], axis=0)), lax.optimization_barrier(jnp.sum(mixer[7], axis=0)), attention[0], attention[1], attention[2], attention[3])
```

```python
import functools

import jax
import jax.numpy as jnp
from jax import lax
from jax.experimental import pallas as pl
from jax.experimental.pallas import tpu as pltpu
from jax.sharding import PartitionSpec as P

NS = 16
HEAD = 128
BLOCK = 32
LANES = 128
SEGS = 8
RESET = 1e30
LOG2E = 1.4426950408889634
NEG = -1e30
KEYS = 256
SUMMARY_ROWS = 48

F32 = jnp.float32
BF16 = jnp.bfloat16


def dot(a, b, dims=((1,), (0,)), precision=None):
    return lax.dot_general(a, b, (dims, ((), ())), precision=precision, preferred_element_type=F32)


def exact_dot(a, b, dims=((1,), (0,))):
    return dot(a, b, dims, lax.Precision.HIGHEST)


def iota(shape, axis):
    return lax.broadcasted_iota(jnp.int32, shape, axis)


def to_segments(tokens):
    span = tokens // SEGS
    row = iota((tokens, tokens), 0)
    token = iota((tokens, tokens), 1)
    return jnp.where(token == lax.rem(row, SEGS) * span + lax.div(row, SEGS), 1.0, 0.0)


def to_tokens(tokens):
    span = tokens // SEGS
    token = iota((tokens, tokens), 0)
    row = iota((tokens, tokens), 1)
    return jnp.where(row == lax.rem(token, span) * SEGS + lax.div(token, span), 1.0, 0.0)


def starts_of(lengths_ref):
    starts = [jnp.int32(0)]
    for k in range(lengths_ref.shape[0] - 1):
        starts.append(starts[-1] + lengths_ref[k])
    return starts


def softplus_of(raw):
    small = jnp.exp(-jnp.abs(raw))
    one = 1.0 + small
    tail = one - 1.0
    safe = jnp.where(tail == 0.0, 1.0, tail)
    log1p = jnp.where(tail == 0.0, small, jnp.log(one) * (small / safe))
    return jnp.maximum(raw, 0.0) + log1p


def step_sizes(own_ref, lengths_ref, segment, dt_ref, bias_ref, tokens):
    raw = dot(segment, dt_ref[...]) + bias_ref[...]
    delta = softplus_of(raw)
    span = tokens // SEGS
    row = iota(delta.shape, 0)
    token = own_ref[0] * tokens + lax.rem(row, SEGS) * span + lax.div(row, SEGS)
    first = token == 0
    for start in starts_of(lengths_ref):
        first = first | (token == start)
    return raw, delta, jnp.where(first, RESET, delta)


def spread(source, target):
    for n in range(NS):
        target[n] = jnp.broadcast_to(source[n : n + 1], target.shape[1:])


def fill_columns(segment, b_ref, c_ref, b_wide, c_wide):
    tokens = segment.shape[0]
    for source, target in ((b_ref, b_wide), (c_ref, c_wide)):
        columns = dot(segment, source[...], ((1,), (1,)))
        for n in range(NS):
            target[n] = jnp.broadcast_to(columns[:, n : n + 1], (tokens, LANES))


def shifted(value, by, fill):
    rows = value.shape[0]
    row = iota(value.shape, 0)
    moved = pltpu.roll(value, by % rows, 0)
    return jnp.where((row >= by) & (row < rows + by), moved, fill)


def summary_kernel(
    own_ref, lengths_ref, x_ref, dt_ref, dy_ref, b_ref, c_ref, a_ref, bias_ref,
    summary_ref, seg_state_ref, seg_adjoint_ref, seg_delta_ref,
    rate2_ref, b_wide, c_wide, decay_delta, drive, upstream, before_ref, after_ref,
):
    tokens, width = x_ref.shape
    span = tokens // SEGS
    segment = to_segments(tokens).astype(BF16)
    spread(-jnp.exp(a_ref[...]) * LOG2E, rate2_ref)
    raw, delta, reset_delta = step_sizes(own_ref, lengths_ref, segment, dt_ref, bias_ref, tokens)
    decay_delta[...] = reset_delta
    drive[...] = delta * dot(segment, x_ref[...])
    upstream[...] = dot(segment, dy_ref[...])
    fill_columns(segment, b_ref, c_ref, b_wide, c_wide)

    total = reset_delta[:SEGS]
    for pos in range(1, span):
        total = total + reset_delta[pos * SEGS : (pos + 1) * SEGS]
    seg_delta_ref[...] = total
    after = shifted(total, -1, 0.0)
    before = shifted(total, 1, 0.0)
    for by in (1, 2, 4):
        after = after + shifted(after, -by, 0.0)
        before = before + shifted(before, by, 0.0)
    after_ref[...] = after
    before_ref[...] = before
    whole = before[SEGS - 1 :] + total[SEGS - 1 :]
    high = whole.astype(BF16)
    low = (whole - high.astype(F32)).astype(BF16)
    summary_ref[2 * NS :] = jnp.zeros((SUMMARY_ROWS - 2 * NS, width), BF16)
    summary_ref[2 * NS : 2 * NS + 1] = high
    summary_ref[2 * NS + 1 : 2 * NS + 2] = low

    def state_row(n, carry):
        state_rows, adjoint_rows = [], []
        for lane in range(0, width, LANES):
            cols = slice(lane, lane + LANES)
            rate2 = rate2_ref[n, :, cols]
            state = jnp.zeros((SEGS, LANES), F32)
            decays = []
            for pos in range(span):
                rows = slice(pos * SEGS, (pos + 1) * SEGS)
                decay = jnp.exp2(rate2 * decay_delta[rows, cols])
                decays.append(decay)
                state = decay * state + b_wide[n, rows] * drive[rows, cols]
            adjoint = jnp.zeros((SEGS, LANES), F32)
            for pos in reversed(range(span)):
                rows = slice(pos * SEGS, (pos + 1) * SEGS)
                adjoint = decays[pos] * (c_wide[n, rows] * upstream[rows, cols] + adjoint)
            seg_state_ref[n, :, cols] = state
            seg_adjoint_ref[n, :, cols] = adjoint
            weight = jnp.exp2(rate2 * after_ref[:, cols])
            state_rows.append(jnp.sum(weight * state, axis=0, keepdims=True))
            weight = jnp.exp2(rate2 * before_ref[:, cols])
            adjoint_rows.append(jnp.sum(weight * adjoint, axis=0, keepdims=True))
        sel = iota((NS, width), 0) == n
        states, adjoints = carry
        states = jnp.where(sel, jnp.concatenate(state_rows, 1), states)
        adjoints = jnp.where(sel, jnp.concatenate(adjoint_rows, 1), adjoints)
        return states, adjoints

    zero = jnp.zeros((NS, width), F32)
    states, adjoints = lax.fori_loop(0, NS, state_row, (zero, zero))
    summary_ref[:NS] = states.astype(BF16)
    summary_ref[NS : 2 * NS] = adjoints.astype(BF16)


def mixer_kernel(
    own_ref, lengths_ref, x_ref, dt_ref, dy_ref, b_ref, c_ref, a_ref, bias_ref, skip_ref,
    summaries_ref, seg_state_ref, seg_adjoint_ref, seg_delta_ref,
    out_ref, x_grad_ref, dt_grad_ref, bc_ref, params_ref,
    rate_ref, rate2_ref, b_wide, c_wide, delta_ref, decay_delta, drive, upstream,
    enter_ref, arrive_ref, y_acc, xg_acc, dd_acc, bg_acc, cg_acc, rate_acc,
):
    tokens, width = x_ref.shape
    span = tokens // SEGS
    count = summaries_ref.shape[0]
    own = own_ref[0]
    segment = to_segments(tokens).astype(BF16)
    rate_all = -jnp.exp(a_ref[...])
    rate2_all = rate_all * LOG2E
    spread(rate_all, rate_ref)
    spread(rate2_all, rate2_ref)
    raw, delta, reset_delta = step_sizes(own_ref, lengths_ref, segment, dt_ref, bias_ref, tokens)
    delta_ref[...] = delta
    decay_delta[...] = reset_delta
    inputs = dot(segment, x_ref[...])
    drive[...] = delta * inputs
    upstream[...] = dot(segment, dy_ref[...])
    fill_columns(segment, b_ref, c_ref, b_wide, c_wide)

    entering = jnp.zeros((NS, width), F32)
    arriving = jnp.zeros((NS, width), F32)

    def factor(j):
        ends = summaries_ref[j, 2 * NS : 2 * NS + 2].astype(F32)
        return jnp.exp2(rate2_all * (ends[0:1] + ends[1:2]))

    for j in range(count - 1):
        longer = factor(j) * entering + summaries_ref[j, :NS].astype(F32)
        entering = jnp.where(j < own, longer, entering)
    for j in reversed(range(1, count)):
        longer = factor(j) * arriving + summaries_ref[j, NS : 2 * NS].astype(F32)
        arriving = jnp.where(j > own, longer, arriving)
    spread(entering, enter_ref)
    spread(arriving, arrive_ref)

    y_acc[...] = jnp.zeros_like(y_acc)
    xg_acc[...] = jnp.zeros_like(xg_acc)
    dd_acc[...] = jnp.zeros_like(dd_acc)

    def state_row(n, carry):
        for lane in range(0, width, LANES):
            cols = slice(lane, lane + LANES)
            rate = rate_ref[n, :, cols]
            rate2 = rate2_ref[n, :, cols]
            row = iota((SEGS, LANES), 0)
            seg_factor = jnp.exp2(rate2 * seg_delta_ref[:, cols])
            edge = enter_ref[n, :, cols]
            scale, total = seg_factor, seg_state_ref[n, :, cols]
            for by in (1, 2, 4):
                total = total + scale * shifted(total, by, 0.0)
                scale = scale * shifted(scale, by, 1.0)
            state = jnp.where(row == 0, edge, pltpu.roll(total + scale * edge, 1, 0))
            edge = arrive_ref[n, :, cols]
            scale, total = seg_factor, seg_adjoint_ref[n, :, cols]
            for by in (1, 2, 4):
                total = total + scale * shifted(total, -by, 0.0)
                scale = scale * shifted(scale, -by, 1.0)
            moved = pltpu.roll(total + scale * edge, SEGS - 1, 0)
            adjoint = jnp.where(row == SEGS - 1, edge, moved)
            decays, befores = [], []
            for pos in range(span):
                rows = slice(pos * SEGS, (pos + 1) * SEGS)
                decay = jnp.exp2(rate2 * decay_delta[rows, cols])
                decays.append(decay)
                befores.append(state)
                state = decay * state + b_wide[n, rows] * drive[rows, cols]
                y_acc[rows, cols] += c_wide[n, rows] * state
                part = upstream[rows, cols] * state
                if lane == 0:
                    cg_acc[n, rows] = part
                else:
                    cg_acc[n, rows] += part
            rate_sum = jnp.zeros((SEGS, LANES), F32)
            for pos in reversed(range(span)):
                rows = slice(pos * SEGS, (pos + 1) * SEGS)
                full = c_wide[n, rows] * upstream[rows, cols] + adjoint
                adjoint = decays[pos] * full
                xg_acc[rows, cols] += full * b_wide[n, rows]
                part = full * drive[rows, cols]
                if lane == 0:
                    bg_acc[n, rows] = part
                else:
                    bg_acc[n, rows] += part
                through = adjoint * befores[pos]
                dd_acc[rows, cols] += rate * through
                rate_sum = rate_sum + delta_ref[rows, cols] * through
            rate_acc[n, :, cols] = rate * rate_sum
        return carry

    lax.fori_loop(0, NS, state_row, 0)

    token = to_tokens(tokens).astype(BF16)
    inputs = dot(segment, x_ref[...])
    skip = skip_ref[...]
    out_ref[...] = dot(token, (y_acc[...] + skip * inputs).astype(BF16)).astype(BF16)
    x_grad = xg_acc[...] * delta_ref[...] + skip * upstream[...]
    x_grad_ref[...] = dot(token, x_grad.astype(BF16)).astype(BF16)
    raw = dot(segment, dt_ref[...]) + bias_ref[...]
    raw_grad = (xg_acc[...] * inputs + dd_acc[...]) / (1.0 + jnp.exp(-raw))
    dt_grad_ref[...] = dot(token, raw_grad.astype(BF16)).astype(BF16)
    params_ref[:NS] = jnp.sum(rate_acc[...], axis=1)
    params_ref[NS : NS + 1] = jnp.sum(upstream[...] * inputs, axis=0, keepdims=True)
    params_ref[NS + 1 : NS + 2] = jnp.sum(raw_grad, axis=0, keepdims=True)
    ones = jnp.ones((SEGS, LANES), F32)
    sums = []
    for source in (bg_acc, cg_acc):
        for n in range(NS):
            sums.append(exact_dot(ones, source[n], ((1,), (1,)))[:1])
    bc_ref[...] = exact_dot(jnp.concatenate(sums, 0), to_segments(tokens))


def attention_kernel(
    own_ref, lengths_ref, plan_ref, all_ref, dout_ref,
    out_ref, query_grad_ref, kv_grad_ref,
    query_t, dout_t, score_ref, turned, out_acc, query_acc,
):
    tokens, width = dout_ref.shape
    rows_all = all_ref.shape[0]
    heads = width // HEAD
    columns = heads * tokens
    places = tokens // BLOCK
    factor = (HEAD ** -0.5) * LOG2E
    starts = starts_of(lengths_ref)
    wanted = [plan_ref[own_ref[0] * places + p] for p in range(places)]

    picked = jnp.concatenate(
        [all_ref[pl.ds(pl.multiple_of(w * BLOCK, BLOCK), BLOCK), :width] for w in wanted], 0
    )
    dout = dout_ref[...]
    query = jnp.concatenate([picked[:, h * HEAD : (h + 1) * HEAD] for h in range(heads)], 0)
    d_att = jnp.concatenate([dout[:, h * HEAD : (h + 1) * HEAD] for h in range(heads)], 0)
    query_t[...] = query.astype(F32).T.astype(BF16)
    dout_t[...] = d_att.astype(F32).T.astype(BF16)

    column = lax.rem(iota((1, columns), 1), tokens)
    place = lax.div(column, BLOCK)
    block = jnp.zeros((1, columns), jnp.int32)
    for p, w in enumerate(wanted):
        block = jnp.where(place == p, w, block)
    last = block * BLOCK + lax.rem(column, BLOCK)
    opening = jnp.zeros((1, columns), jnp.int32)
    for start in starts:
        opening = jnp.where(start <= last, start, opening)

    lowest = jnp.int32(rows_all)
    highest = jnp.int32(0)
    for w in wanted:
        low = jnp.int32(0)
        for start in starts:
            low = jnp.where(start <= w * BLOCK, start, low)
        lowest = jnp.minimum(lowest, low)
        highest = jnp.maximum(highest, w * BLOCK + BLOCK)
    begin = lax.div(lowest, KEYS)
    end = lax.div(highest + KEYS - 1, KEYS)

    def at(j):
        return pl.ds(pl.multiple_of(j * KEYS, KEYS), KEYS)

    def score_step(j, top):
        scores = dot(all_ref[at(j), width : width + HEAD], query_t[...])
        key = j * KEYS + iota((KEYS, columns), 0)
        scores = jnp.where((key <= last) & (key >= opening), scores, NEG)
        score_ref[at(j)] = scores
        return jnp.maximum(top, jnp.max(scores.reshape(KEYS // 8, 8, columns), axis=0))

    top = lax.fori_loop(begin, end, score_step, jnp.full((8, columns), NEG, F32))
    shift = jnp.max(top, axis=0, keepdims=True) * factor

    out_acc[...] = jnp.zeros_like(out_acc)

    def weight_step(j, total):
        weights = jnp.exp2(score_ref[at(j)] * factor - shift)
        score_ref[at(j)] = weights
        value_t = all_ref[at(j), width + HEAD :].astype(F32).T.astype(BF16)
        out_acc[...] += dot(value_t, weights.astype(BF16))
        return total + jnp.sum(weights.reshape(KEYS // 8, 8, columns), axis=0)

    total = lax.fori_loop(begin, end, weight_step, jnp.zeros((8, columns), F32))
    inverse = 1.0 / jnp.sum(total, axis=0, keepdims=True)
    attended = (out_acc[...] * inverse).astype(BF16)
    rowdot = jnp.sum(attended.astype(F32) * dout_t[...].astype(F32), axis=0, keepdims=True)
    turned[...] = attended.astype(F32).T
    for h in range(heads):
        out_ref[:, h * HEAD : (h + 1) * HEAD] = turned[h * tokens : (h + 1) * tokens].astype(BF16)

    query_acc[...] = jnp.zeros_like(query_acc)
    kv_grad_ref[...] = jnp.zeros_like(kv_grad_ref)

    def gradient_step(j, carry):
        keys = all_ref[at(j), width : width + HEAD]
        d_probs = dot(all_ref[at(j), width + HEAD :], dout_t[...])
        probs = score_ref[at(j)] * inverse
        d_scores = (probs * (d_probs - rowdot)).astype(BF16)
        query_acc[...] += dot(keys.astype(F32).T.astype(BF16), d_scores)
        key_grad = dot(d_scores, query) * (HEAD ** -0.5)
        value_grad = dot(probs.astype(BF16), d_att)
        kv_grad_ref[at(j), :HEAD] = key_grad.astype(BF16)
        kv_grad_ref[at(j), HEAD:] = value_grad.astype(BF16)
        return carry

    lax.fori_loop(begin, end, gradient_step, 0)
    turned[...] = (query_acc[...] * (HEAD ** -0.5)).T
    for h in range(heads):
        query_grad_ref[:, h * HEAD : (h + 1) * HEAD] = turned[
            h * tokens : (h + 1) * tokens
        ].astype(BF16)


VMEM = pl.BlockSpec(memory_space=pltpu.VMEM)
SMEM = pl.BlockSpec(memory_space=pltpu.SMEM)
PARAMS = pltpu.CompilerParams(vmem_limit_bytes=48 * 1024 * 1024)


def shape(dims, dtype):
    return jax.ShapeDtypeStruct(dims, dtype)


def on_device(
    x_in, dt_in, b_in, c_in, dy_in, a_log, d_skip, dt_bias,
    q_in, k_in, value_input, dout_in, doc_lengths, plan,
):
    seq_count = lax.axis_size("seq")
    own = lax.axis_index("seq").astype(jnp.int32).reshape(1)
    tokens, width = x_in.shape[1:]
    row_tokens = tokens * seq_count
    lengths = doc_lengths[0]
    x, dt, dy, b, c = x_in[0], dt_in[0], dy_in[0], b_in[0], c_in[0]
    bias, skip = dt_bias[None], d_skip[None]

    mixed = jnp.concatenate([q_in[0], k_in[0], value_input[0]], axis=1)
    gathered = lax.all_gather(mixed, "seq", axis=0, tiled=True)

    wide = functools.partial(pltpu.VMEM, dtype=F32)
    seg_shape = shape((NS, SEGS, width), F32)
    summary, seg_state, seg_adjoint, seg_delta = pl.pallas_call(
        summary_kernel,
        out_shape=(
            shape((SUMMARY_ROWS, width), BF16), seg_shape, seg_shape, shape((SEGS, width), F32),
        ),
        in_specs=[SMEM] * 2 + [VMEM] * 7,
        out_specs=[VMEM] * 4,
        scratch_shapes=[
            wide((NS, SEGS, width)),
            wide((NS, tokens, LANES)), wide((NS, tokens, LANES)),
            wide((tokens, width)), wide((tokens, width)), wide((tokens, width)),
            wide((SEGS, width)), wide((SEGS, width)),
        ],
        compiler_params=PARAMS,
        name="mixer_summary",
    )(own, lengths, x, dt, dy, b, c, a_log, bias)
    summaries = lax.all_gather(summary, "seq", axis=0)

    output, x_grad, dt_grad, bc_part, params_part = pl.pallas_call(
        mixer_kernel,
        out_shape=(
            shape((tokens, width), BF16), shape((tokens, width), BF16),
            shape((tokens, width), BF16), shape((2 * NS, tokens), F32),
            shape((NS + 2, width), F32),
        ),
        in_specs=[SMEM] * 2 + [VMEM] * 12,
        out_specs=[VMEM] * 5,
        scratch_shapes=[
            wide((NS, SEGS, width)), wide((NS, SEGS, width)),
            wide((NS, tokens, LANES)), wide((NS, tokens, LANES)),
            wide((tokens, width)), wide((tokens, width)),
            wide((tokens, width)), wide((tokens, width)),
            wide((NS, SEGS, width)), wide((NS, SEGS, width)),
            wide((tokens, width)), wide((tokens, width)), wide((tokens, width)),
            wide((NS, tokens, LANES)), wide((NS, tokens, LANES)),
            wide((NS, SEGS, width)),
        ],
        compiler_params=PARAMS,
        name="mixer",
    )(
        own, lengths, x, dt, dy, b, c, a_log, bias, skip,
        summaries, seg_state, seg_adjoint, seg_delta,
    )
    bc_sum = lax.psum(bc_part, "tp")
    params_row = lax.psum(params_part, "dp")
    params_sum = jnp.sum(lax.all_gather(params_row, "seq", axis=0), axis=0)

    attn_out, query_gradient, kv_part = pl.pallas_call(
        attention_kernel,
        out_shape=(
            shape((tokens, width), BF16), shape((tokens, width), BF16),
            shape((row_tokens, 2 * HEAD), BF16),
        ),
        in_specs=[SMEM] * 3 + [VMEM] * 2,
        out_specs=[VMEM] * 3,
        scratch_shapes=[
            pltpu.VMEM((HEAD, width // HEAD * tokens), BF16),
            pltpu.VMEM((HEAD, width // HEAD * tokens), BF16),
            wide((row_tokens, width // HEAD * tokens)),
            wide((width // HEAD * tokens, HEAD)),
            wide((HEAD, width // HEAD * tokens)),
            wide((HEAD, width // HEAD * tokens)),
        ],
        compiler_params=PARAMS,
        name="attention",
    )(own, lengths, plan[0], gathered, dout_in[0])
    kv_parts = lax.all_to_all(
        kv_part.reshape(seq_count, tokens, 2 * HEAD), "seq", split_axis=0, concat_axis=0
    )
    kv_sum = jnp.sum(kv_parts.astype(F32), axis=0).astype(BF16)
    return (
        output[None],
        x_grad[None],
        dt_grad[None],
        bc_sum[None, :NS],
        bc_sum[None, NS:],
        params_sum[:NS],
        params_sum[NS],
        params_sum[NS + 1],
        attn_out[None],
        query_gradient[None],
        kv_sum[None, :, :HEAD],
        kv_sum[None, :, HEAD:],
    )


def solution(mesh):
    tokens = P("dp", "seq", "tp")
    columns = P("dp", None, "seq")
    row = P("dp", None)
    return jax.shard_map(
        on_device,
        mesh=mesh,
        in_specs=(
            tokens, tokens, columns, columns, tokens, P(None, "tp"), P("tp"), P("tp"),
            tokens, tokens, tokens, tokens, row, row,
        ),
        out_specs=(
            tokens, tokens, tokens, columns, columns, P(None, "tp"), P("tp"), P("tp"),
            tokens, tokens, tokens, tokens,
        ),
        check_vma=False,
    )
```

```python
import functools

import jax
import jax.numpy as jnp
from jax import lax
from jax.experimental import pallas as pl
from jax.experimental.pallas import tpu as pltpu
from jax.sharding import PartitionSpec as P

NS = 16
HEAD = 128
BLOCK = 32
LANES = 128
SEGS = 8
RESET = 1e30
LOG2E = 1.4426950408889634
NEG = -1e30
KEYS = 256
SUMMARY_ROWS = 48

F32 = jnp.float32
BF16 = jnp.bfloat16


def dot(a, b, dims=((1,), (0,)), precision=None):
    return lax.dot_general(a, b, (dims, ((), ())), precision=precision, preferred_element_type=F32)


def exact_dot(a, b, dims=((1,), (0,))):
    return dot(a, b, dims, lax.Precision.HIGHEST)


def iota(shape, axis):
    return lax.broadcasted_iota(jnp.int32, shape, axis)


def to_segments(tokens):
    span = tokens // SEGS
    row = iota((tokens, tokens), 0)
    token = iota((tokens, tokens), 1)
    return jnp.where(token == lax.rem(row, SEGS) * span + lax.div(row, SEGS), 1.0, 0.0)


def to_tokens(tokens):
    span = tokens // SEGS
    token = iota((tokens, tokens), 0)
    row = iota((tokens, tokens), 1)
    return jnp.where(row == lax.rem(token, span) * SEGS + lax.div(token, span), 1.0, 0.0)


def starts_of(lengths_ref):
    starts = [jnp.int32(0)]
    for k in range(lengths_ref.shape[0] - 1):
        starts.append(starts[-1] + lengths_ref[k])
    return starts


def softplus_of(raw):
    small = jnp.exp(-jnp.abs(raw))
    one = 1.0 + small
    tail = one - 1.0
    safe = jnp.where(tail == 0.0, 1.0, tail)
    log1p = jnp.where(tail == 0.0, small, jnp.log(one) * (small / safe))
    return jnp.maximum(raw, 0.0) + log1p


def step_sizes(own_ref, lengths_ref, segment, dt_ref, bias_ref, tokens):
    raw = dot(segment, dt_ref[...]) + bias_ref[...]
    delta = softplus_of(raw)
    span = tokens // SEGS
    row = iota(delta.shape, 0)
    token = own_ref[0] * tokens + lax.rem(row, SEGS) * span + lax.div(row, SEGS)
    first = token == 0
    for start in starts_of(lengths_ref):
        first = first | (token == start)
    return raw, delta, jnp.where(first, RESET, delta)


def spread(source, target):
    for n in range(NS):
        target[n] = jnp.broadcast_to(source[n : n + 1], target.shape[1:])


def fill_columns(segment, b_ref, c_ref, b_wide, c_wide):
    tokens = segment.shape[0]
    for source, target in ((b_ref, b_wide), (c_ref, c_wide)):
        columns = dot(segment, source[...], ((1,), (1,)))
        for n in range(NS):
            target[n] = jnp.broadcast_to(columns[:, n : n + 1], (tokens, LANES))


def shifted(value, by, fill):
    rows = value.shape[0]
    row = iota(value.shape, 0)
    moved = pltpu.roll(value, by % rows, 0)
    return jnp.where((row >= by) & (row < rows + by), moved, fill)


def summary_kernel(
    own_ref, lengths_ref, x_ref, dt_ref, dy_ref, b_ref, c_ref, a_ref, bias_ref,
    summary_ref, seg_state_ref, seg_adjoint_ref, seg_delta_ref,
    rate2_ref, b_wide, c_wide, decay_delta, drive, upstream, before_ref, after_ref,
):
    tokens, width = x_ref.shape
    span = tokens // SEGS
    segment = to_segments(tokens).astype(BF16)
    spread(-jnp.exp(a_ref[...]) * LOG2E, rate2_ref)
    raw, delta, reset_delta = step_sizes(own_ref, lengths_ref, segment, dt_ref, bias_ref, tokens)
    decay_delta[...] = reset_delta
    drive[...] = delta * dot(segment, x_ref[...])
    upstream[...] = dot(segment, dy_ref[...])
    fill_columns(segment, b_ref, c_ref, b_wide, c_wide)

    total = reset_delta[:SEGS]
    for pos in range(1, span):
        total = total + reset_delta[pos * SEGS : (pos + 1) * SEGS]
    seg_delta_ref[...] = total
    after = shifted(total, -1, 0.0)
    before = shifted(total, 1, 0.0)
    for by in (1, 2, 4):
        after = after + shifted(after, -by, 0.0)
        before = before + shifted(before, by, 0.0)
    after_ref[...] = after
    before_ref[...] = before
    whole = before[SEGS - 1 :] + total[SEGS - 1 :]
    high = whole.astype(BF16)
    low = (whole - high.astype(F32)).astype(BF16)
    summary_ref[2 * NS :] = jnp.zeros((SUMMARY_ROWS - 2 * NS, width), BF16)
    summary_ref[2 * NS : 2 * NS + 1] = high
    summary_ref[2 * NS + 1 : 2 * NS + 2] = low

    def state_row(n, carry):
        state_rows, adjoint_rows = [], []
        for lane in range(0, width, LANES):
            cols = slice(lane, lane + LANES)
            rate2 = rate2_ref[n, :, cols]
            state = jnp.zeros((SEGS, LANES), F32)
            decays = []
            for pos in range(span):
                rows = slice(pos * SEGS, (pos + 1) * SEGS)
                decay = jnp.exp2(rate2 * decay_delta[rows, cols])
                decays.append(decay)
                state = decay * state + b_wide[n, rows] * drive[rows, cols]
            adjoint = jnp.zeros((SEGS, LANES), F32)
            for pos in reversed(range(span)):
                rows = slice(pos * SEGS, (pos + 1) * SEGS)
                adjoint = decays[pos] * (c_wide[n, rows] * upstream[rows, cols] + adjoint)
            seg_state_ref[n, :, cols] = state
            seg_adjoint_ref[n, :, cols] = adjoint
            weight = jnp.exp2(rate2 * after_ref[:, cols])
            state_rows.append(jnp.sum(weight * state, axis=0, keepdims=True))
            weight = jnp.exp2(rate2 * before_ref[:, cols])
            adjoint_rows.append(jnp.sum(weight * adjoint, axis=0, keepdims=True))
        sel = iota((NS, width), 0) == n
        states, adjoints = carry
        states = jnp.where(sel, jnp.concatenate(state_rows, 1), states)
        adjoints = jnp.where(sel, jnp.concatenate(adjoint_rows, 1), adjoints)
        return states, adjoints

    zero = jnp.zeros((NS, width), F32)
    states, adjoints = lax.fori_loop(0, NS, state_row, (zero, zero))
    summary_ref[:NS] = states.astype(BF16)
    summary_ref[NS : 2 * NS] = adjoints.astype(BF16)


def mixer_kernel(
    own_ref, lengths_ref, x_ref, dt_ref, dy_ref, b_ref, c_ref, a_ref, bias_ref, skip_ref,
    summaries_ref, seg_state_ref, seg_adjoint_ref, seg_delta_ref,
    out_ref, x_grad_ref, dt_grad_ref, bc_ref, params_ref,
    rate_ref, rate2_ref, b_wide, c_wide, delta_ref, decay_delta, drive, upstream,
    enter_ref, arrive_ref, y_acc, xg_acc, dd_acc, bg_acc, cg_acc, rate_acc,
):
    tokens, width = x_ref.shape
    span = tokens // SEGS
    count = summaries_ref.shape[0]
    own = own_ref[0]
    segment = to_segments(tokens).astype(BF16)
    rate_all = -jnp.exp(a_ref[...])
    rate2_all = rate_all * LOG2E
    spread(rate_all, rate_ref)
    spread(rate2_all, rate2_ref)
    raw, delta, reset_delta = step_sizes(own_ref, lengths_ref, segment, dt_ref, bias_ref, tokens)
    delta_ref[...] = delta
    decay_delta[...] = reset_delta
    inputs = dot(segment, x_ref[...])
    drive[...] = delta * inputs
    upstream[...] = dot(segment, dy_ref[...])
    fill_columns(segment, b_ref, c_ref, b_wide, c_wide)

    entering = jnp.zeros((NS, width), F32)
    arriving = jnp.zeros((NS, width), F32)

    def factor(j):
        ends = summaries_ref[j, 2 * NS : 2 * NS + 2].astype(F32)
        return jnp.exp2(rate2_all * (ends[0:1] + ends[1:2]))

    for j in range(count - 1):
        longer = factor(j) * entering + summaries_ref[j, :NS].astype(F32)
        entering = jnp.where(j < own, longer, entering)
    for j in reversed(range(1, count)):
        longer = factor(j) * arriving + summaries_ref[j, NS : 2 * NS].astype(F32)
        arriving = jnp.where(j > own, longer, arriving)
    spread(entering, enter_ref)
    spread(arriving, arrive_ref)

    y_acc[...] = jnp.zeros_like(y_acc)
    xg_acc[...] = jnp.zeros_like(xg_acc)
    dd_acc[...] = jnp.zeros_like(dd_acc)

    def state_row(n, carry):
        for lane in range(0, width, LANES):
            cols = slice(lane, lane + LANES)
            rate = rate_ref[n, :, cols]
            rate2 = rate2_ref[n, :, cols]
            row = iota((SEGS, LANES), 0)
            seg_factor = jnp.exp2(rate2 * seg_delta_ref[:, cols])
            edge = enter_ref[n, :, cols]
            scale, total = seg_factor, seg_state_ref[n, :, cols]
            for by in (1, 2, 4):
                total = total + scale * shifted(total, by, 0.0)
                scale = scale * shifted(scale, by, 1.0)
            state = jnp.where(row == 0, edge, pltpu.roll(total + scale * edge, 1, 0))
            edge = arrive_ref[n, :, cols]
            scale, total = seg_factor, seg_adjoint_ref[n, :, cols]
            for by in (1, 2, 4):
                total = total + scale * shifted(total, -by, 0.0)
                scale = scale * shifted(scale, -by, 1.0)
            moved = pltpu.roll(total + scale * edge, SEGS - 1, 0)
            adjoint = jnp.where(row == SEGS - 1, edge, moved)
            decays, befores = [], []
            for pos in range(span):
                rows = slice(pos * SEGS, (pos + 1) * SEGS)
                decay = jnp.exp2(rate2 * decay_delta[rows, cols])
                decays.append(decay)
                befores.append(state)
                state = decay * state + b_wide[n, rows] * drive[rows, cols]
                y_acc[rows, cols] += c_wide[n, rows] * state
                part = upstream[rows, cols] * state
                if lane == 0:
                    cg_acc[n, rows] = part
                else:
                    cg_acc[n, rows] += part
            rate_sum = jnp.zeros((SEGS, LANES), F32)
            for pos in reversed(range(span)):
                rows = slice(pos * SEGS, (pos + 1) * SEGS)
                full = c_wide[n, rows] * upstream[rows, cols] + adjoint
                adjoint = decays[pos] * full
                xg_acc[rows, cols] += full * b_wide[n, rows]
                part = full * drive[rows, cols]
                if lane == 0:
                    bg_acc[n, rows] = part
                else:
                    bg_acc[n, rows] += part
                through = adjoint * befores[pos]
                dd_acc[rows, cols] += rate * through
                rate_sum = rate_sum + delta_ref[rows, cols] * through
            rate_acc[n, :, cols] = rate * rate_sum
        return carry

    lax.fori_loop(0, NS, state_row, 0)

    token = to_tokens(tokens).astype(BF16)
    inputs = dot(segment, x_ref[...])
    skip = skip_ref[...]
    out_ref[...] = dot(token, (y_acc[...] + skip * inputs).astype(BF16)).astype(BF16)
    x_grad = xg_acc[...] * delta_ref[...] + skip * upstream[...]
    x_grad_ref[...] = dot(token, x_grad.astype(BF16)).astype(BF16)
    raw = dot(segment, dt_ref[...]) + bias_ref[...]
    raw_grad = (xg_acc[...] * inputs + dd_acc[...]) / (1.0 + jnp.exp(-raw))
    dt_grad_ref[...] = dot(token, raw_grad.astype(BF16)).astype(BF16)
    params_ref[:NS] = jnp.sum(rate_acc[...], axis=1)
    params_ref[NS : NS + 1] = jnp.sum(upstream[...] * inputs, axis=0, keepdims=True)
    params_ref[NS + 1 : NS + 2] = jnp.sum(raw_grad, axis=0, keepdims=True)
    ones = jnp.ones((SEGS, LANES), F32)
    sums = []
    for source in (bg_acc, cg_acc):
        for n in range(NS):
            sums.append(exact_dot(ones, source[n], ((1,), (1,)))[:1])
    bc_ref[...] = exact_dot(jnp.concatenate(sums, 0), to_segments(tokens))


def attention_kernel(
    own_ref, lengths_ref, plan_ref, all_ref, dout_ref,
    out_ref, query_grad_ref, kv_grad_ref,
    query_t, dout_t, score_ref, turned, out_acc, query_acc,
):
    tokens, width = dout_ref.shape
    rows_all = all_ref.shape[0]
    heads = width // HEAD
    columns = heads * tokens
    places = tokens // BLOCK
    factor = (HEAD ** -0.5) * LOG2E
    starts = starts_of(lengths_ref)
    wanted = [plan_ref[own_ref[0] * places + p] for p in range(places)]

    picked = jnp.concatenate(
        [all_ref[pl.ds(pl.multiple_of(w * BLOCK, BLOCK), BLOCK), :width] for w in wanted], 0
    )
    dout = dout_ref[...]
    query = jnp.concatenate([picked[:, h * HEAD : (h + 1) * HEAD] for h in range(heads)], 0)
    d_att = jnp.concatenate([dout[:, h * HEAD : (h + 1) * HEAD] for h in range(heads)], 0)
    query_t[...] = query.astype(F32).T.astype(BF16)
    dout_t[...] = d_att.astype(F32).T.astype(BF16)

    column = lax.rem(iota((1, columns), 1), tokens)
    place = lax.div(column, BLOCK)
    block = jnp.zeros((1, columns), jnp.int32)
    for p, w in enumerate(wanted):
        block = jnp.where(place == p, w, block)
    last = block * BLOCK + lax.rem(column, BLOCK)
    opening = jnp.zeros((1, columns), jnp.int32)
    for start in starts:
        opening = jnp.where(start <= last, start, opening)

    lowest = jnp.int32(rows_all)
    highest = jnp.int32(0)
    for w in wanted:
        low = jnp.int32(0)
        for start in starts:
            low = jnp.where(start <= w * BLOCK, start, low)
        lowest = jnp.minimum(lowest, low)
        highest = jnp.maximum(highest, w * BLOCK + BLOCK)
    begin = lax.div(lowest, KEYS)
    end = lax.div(highest + KEYS - 1, KEYS)

    def at(j):
        return pl.ds(pl.multiple_of(j * KEYS, KEYS), KEYS)

    def score_step(j, top):
        scores = dot(all_ref[at(j), width : width + HEAD], query_t[...])
        key = j * KEYS + iota((KEYS, columns), 0)
        scores = jnp.where((key <= last) & (key >= opening), scores, NEG)
        score_ref[at(j)] = scores
        return jnp.maximum(top, jnp.max(scores.reshape(KEYS // 8, 8, columns), axis=0))

    top = lax.fori_loop(begin, end, score_step, jnp.full((8, columns), NEG, F32))
    shift = jnp.max(top, axis=0, keepdims=True) * factor

    out_acc[...] = jnp.zeros_like(out_acc)

    def weight_step(j, total):
        weights = jnp.exp2(score_ref[at(j)] * factor - shift)
        score_ref[at(j)] = weights
        value_t = all_ref[at(j), width + HEAD :].astype(F32).T.astype(BF16)
        out_acc[...] += dot(value_t, weights.astype(BF16))
        return total + jnp.sum(weights.reshape(KEYS // 8, 8, columns), axis=0)

    total = lax.fori_loop(begin, end, weight_step, jnp.zeros((8, columns), F32))
    inverse = 1.0 / jnp.sum(total, axis=0, keepdims=True)
    attended = (out_acc[...] * inverse).astype(BF16)
    rowdot = jnp.sum(attended.astype(F32) * dout_t[...].astype(F32), axis=0, keepdims=True)
    turned[...] = attended.astype(F32).T
    for h in range(heads):
        out_ref[:, h * HEAD : (h + 1) * HEAD] = turned[h * tokens : (h + 1) * tokens].astype(BF16)

    query_acc[...] = jnp.zeros_like(query_acc)
    kv_grad_ref[...] = jnp.zeros_like(kv_grad_ref)

    def gradient_step(j, carry):
        keys = all_ref[at(j), width : width + HEAD]
        d_probs = dot(all_ref[at(j), width + HEAD :], dout_t[...])
        probs = score_ref[at(j)] * inverse
        d_scores = (probs * (d_probs - rowdot)).astype(BF16)
        query_acc[...] += dot(keys.astype(F32).T.astype(BF16), d_scores)
        key_grad = dot(d_scores, query) * (HEAD ** -0.5)
        value_grad = dot(probs.astype(BF16), d_att)
        kv_grad_ref[at(j), :HEAD] = key_grad.astype(BF16)
        kv_grad_ref[at(j), HEAD:] = value_grad.astype(BF16)
        return carry

    lax.fori_loop(begin, end, gradient_step, 0)
    turned[...] = (query_acc[...] * (HEAD ** -0.5)).T
    for h in range(heads):
        query_grad_ref[:, h * HEAD : (h + 1) * HEAD] = turned[
            h * tokens : (h + 1) * tokens
        ].astype(BF16)


VMEM = pl.BlockSpec(memory_space=pltpu.VMEM)
SMEM = pl.BlockSpec(memory_space=pltpu.SMEM)
PARAMS = pltpu.CompilerParams(vmem_limit_bytes=48 * 1024 * 1024)


def shape(dims, dtype):
    return jax.ShapeDtypeStruct(dims, dtype)


def on_device(
    x_in, dt_in, b_in, c_in, dy_in, a_log, d_skip, dt_bias,
    q_in, k_in, value_input, dout_in, doc_lengths, plan,
):
    seq_count = lax.axis_size("seq")
    own = lax.axis_index("seq").astype(jnp.int32).reshape(1)
    tokens, width = x_in.shape[1:]
    row_tokens = tokens * seq_count
    lengths = doc_lengths[0]
    x, dt, dy, b, c = x_in[0], dt_in[0], dy_in[0], b_in[0], c_in[0]
    bias, skip = dt_bias[None], d_skip[None]

    mixed = jnp.concatenate([q_in[0], k_in[0], value_input[0]], axis=1)
    gathered = lax.all_gather(mixed, "seq", axis=0, tiled=True)

    wide = functools.partial(pltpu.VMEM, dtype=F32)
    seg_shape = shape((NS, SEGS, width), F32)
    summary, seg_state, seg_adjoint, seg_delta = pl.pallas_call(
        summary_kernel,
        out_shape=(
            shape((SUMMARY_ROWS, width), BF16), seg_shape, seg_shape, shape((SEGS, width), F32),
        ),
        in_specs=[SMEM] * 2 + [VMEM] * 7,
        out_specs=[VMEM] * 4,
        scratch_shapes=[
            wide((NS, SEGS, width)),
            wide((NS, tokens, LANES)), wide((NS, tokens, LANES)),
            wide((tokens, width)), wide((tokens, width)), wide((tokens, width)),
            wide((SEGS, width)), wide((SEGS, width)),
        ],
        compiler_params=PARAMS,
        name="mixer_summary",
    )(own, lengths, x, dt, dy, b, c, a_log, bias)
    summaries = lax.all_gather(summary, "seq", axis=0)

    output, x_grad, dt_grad, bc_part, params_part = pl.pallas_call(
        mixer_kernel,
        out_shape=(
            shape((tokens, width), BF16), shape((tokens, width), BF16),
            shape((tokens, width), BF16), shape((2 * NS, tokens), F32),
            shape((NS + 2, width), F32),
        ),
        in_specs=[SMEM] * 2 + [VMEM] * 12,
        out_specs=[VMEM] * 5,
        scratch_shapes=[
            wide((NS, SEGS, width)), wide((NS, SEGS, width)),
            wide((NS, tokens, LANES)), wide((NS, tokens, LANES)),
            wide((tokens, width)), wide((tokens, width)),
            wide((tokens, width)), wide((tokens, width)),
            wide((NS, SEGS, width)), wide((NS, SEGS, width)),
            wide((tokens, width)), wide((tokens, width)), wide((tokens, width)),
            wide((NS, tokens, LANES)), wide((NS, tokens, LANES)),
            wide((NS, SEGS, width)),
        ],
        compiler_params=PARAMS,
        name="mixer",
    )(
        own, lengths, x, dt, dy, b, c, a_log, bias, skip,
        summaries, seg_state, seg_adjoint, seg_delta,
    )
    params_row = jnp.sum(lax.all_gather(params_part, "seq", axis=0), axis=0)
    gathered, params_row = lax.optimization_barrier((gathered, params_row))

    attn_out, query_gradient, kv_part = pl.pallas_call(
        attention_kernel,
        out_shape=(
            shape((tokens, width), BF16), shape((tokens, width), BF16),
            shape((row_tokens, 2 * HEAD), BF16),
        ),
        in_specs=[SMEM] * 3 + [VMEM] * 2,
        out_specs=[VMEM] * 3,
        scratch_shapes=[
            pltpu.VMEM((HEAD, width // HEAD * tokens), BF16),
            pltpu.VMEM((HEAD, width // HEAD * tokens), BF16),
            wide((row_tokens, width // HEAD * tokens)),
            wide((width // HEAD * tokens, HEAD)),
            wide((HEAD, width // HEAD * tokens)),
            wide((HEAD, width // HEAD * tokens)),
        ],
        compiler_params=PARAMS,
        name="attention",
    )(own, lengths, plan[0], gathered, dout_in[0])
    kv_part, bc_part, params_row = lax.optimization_barrier((kv_part, bc_part, params_row))
    kv_parts = lax.all_to_all(
        kv_part.reshape(seq_count, tokens, 2 * HEAD), "seq", split_axis=0, concat_axis=0
    )
    bc_sum = lax.psum(bc_part, "tp")
    params_sum = lax.psum(params_row, "dp")
    kv_sum = jnp.sum(kv_parts.astype(F32), axis=0).astype(BF16)
    return (
        output[None],
        x_grad[None],
        dt_grad[None],
        bc_sum[None, :NS],
        bc_sum[None, NS:],
        params_sum[:NS],
        params_sum[NS],
        params_sum[NS + 1],
        attn_out[None],
        query_gradient[None],
        kv_sum[None, :, :HEAD],
        kv_sum[None, :, HEAD:],
    )


def solution(mesh):
    tokens = P("dp", "seq", "tp")
    columns = P("dp", None, "seq")
    row = P("dp", None)
    return jax.shard_map(
        on_device,
        mesh=mesh,
        in_specs=(
            tokens, tokens, columns, columns, tokens, P(None, "tp"), P("tp"), P("tp"),
            tokens, tokens, tokens, tokens, row, row,
        ),
        out_specs=(
            tokens, tokens, tokens, columns, columns, P(None, "tp"), P("tp"), P("tp"),
            tokens, tokens, tokens, tokens,
        ),
        check_vma=False,
    )
```

```python
import jax
import jax.numpy as jnp
from jax import lax
from jax.experimental import pallas as pl
from jax.experimental.pallas import tpu as pltpu
from jax.sharding import PartitionSpec as P

NS = 16
HEAD = 128
BLOCK = 32
LANES = 128
SEGS = 8
RESET = 1e30
LOG2E = 1.4426950408889634
NEG = -1e30
SUMMARY_ROWS = 48

F32 = jnp.float32
BF16 = jnp.bfloat16


def dot(a, b, dims=((1,), (0,)), precision=None):
    return lax.dot_general(a, b, (dims, ((), ())), precision=precision, preferred_element_type=F32)


def exact_dot(a, b, dims=((1,), (0,))):
    return dot(a, b, dims, lax.Precision.HIGHEST)


def iota(shape, axis):
    return lax.broadcasted_iota(jnp.int32, shape, axis)


def to_segments(tokens):
    span = tokens // SEGS
    row = iota((tokens, tokens), 0)
    token = iota((tokens, tokens), 1)
    return jnp.where(token == lax.rem(row, SEGS) * span + lax.div(row, SEGS), 1.0, 0.0)


def to_tokens(tokens):
    span = tokens // SEGS
    token = iota((tokens, tokens), 0)
    row = iota((tokens, tokens), 1)
    return jnp.where(row == lax.rem(token, span) * SEGS + lax.div(token, span), 1.0, 0.0)


def starts_of(lengths_ref):
    starts = [jnp.int32(0)]
    for k in range(lengths_ref.shape[1] - 1):
        starts.append(starts[-1] + lengths_ref[0, k])
    return starts


def begin_copies(pairs, semaphores):
    copies = [
        pltpu.make_async_copy(source, target, semaphores.at[k])
        for k, (source, target) in enumerate(pairs)
    ]
    for copy in copies:
        copy.start()
    return copies


def wait_all(copies):
    for copy in copies:
        copy.wait()


def softplus_of(raw):
    small = jnp.exp(-jnp.abs(raw))
    one = 1.0 + small
    tail = one - 1.0
    safe = jnp.where(tail == 0.0, 1.0, tail)
    log1p = jnp.where(tail == 0.0, small, jnp.log(one) * (small / safe))
    return jnp.maximum(raw, 0.0) + log1p


def with_resets(own_ref, lengths_ref, delta):
    tokens = delta.shape[0]
    span = tokens // SEGS
    row = iota(delta.shape, 0)
    token = own_ref[0] * tokens + lax.rem(row, SEGS) * span + lax.div(row, SEGS)
    first = token == 0
    for start in starts_of(lengths_ref):
        first = first | (token == start)
    return jnp.where(first, RESET, delta)


def spread(source, target):
    for n in range(NS):
        target[n] = jnp.broadcast_to(source[n : n + 1], target.shape[1:])


def fill_columns(segment, b_ref, c_ref, b_wide, c_wide):
    tokens = segment.shape[0]
    for source, target in ((b_ref, b_wide), (c_ref, c_wide)):
        columns = dot(segment, source[...], ((1,), (1,)))
        for n in range(NS):
            target[n] = jnp.broadcast_to(columns[:, n : n + 1], (tokens, LANES))


def shifted(value, by, fill):
    rows = value.shape[0]
    row = iota(value.shape, 0)
    moved = pltpu.roll(value, by % rows, 0)
    return jnp.where((row >= by) & (row < rows + by), moved, fill)


def summary_kernel(
    own_ref, lengths_hbm, x_hbm, dt_hbm, dy_hbm, b_hbm, c_hbm, a_hbm, bias_hbm,
    summary_ref, seg_state_ref, seg_adjoint_ref, seg_delta_ref,
    lengths_ref, x_ref, dt_ref, dy_ref, b_ref, c_ref, a_ref, bias_ref,
    rate2_ref, b_wide, c_wide, decay_delta, drive, upstream, before_ref, after_ref, rows_ref, semaphores,
):
    tokens, width = x_ref.shape
    span = tokens // SEGS
    copies = begin_copies(
        (
            (dt_hbm.at[0], dt_ref), (bias_hbm, bias_ref), (lengths_hbm, lengths_ref),
            (x_hbm.at[0], x_ref), (dy_hbm.at[0], dy_ref), (a_hbm, a_ref),
            (b_hbm.at[0], b_ref), (c_hbm.at[0], c_ref),
        ),
        semaphores,
    )
    segment = to_segments(tokens).astype(BF16)
    wait_all(copies[:3])
    raw = dot(segment, dt_ref[...]) + bias_ref[...]
    delta = softplus_of(raw)
    reset_delta = with_resets(own_ref, lengths_ref, delta)
    decay_delta[...] = reset_delta
    wait_all(copies[3:])
    drive[...] = delta * dot(segment, x_ref[...])
    upstream[...] = dot(segment, dy_ref[...])
    spread(-jnp.exp(a_ref[...]) * LOG2E, rate2_ref)
    fill_columns(segment, b_ref, c_ref, b_wide, c_wide)

    total = reset_delta[:SEGS]
    for pos in range(1, span):
        total = total + reset_delta[pos * SEGS : (pos + 1) * SEGS]
    seg_delta_ref[...] = total
    after = shifted(total, -1, 0.0)
    before = shifted(total, 1, 0.0)
    for by in (1, 2, 4):
        after = after + shifted(after, -by, 0.0)
        before = before + shifted(before, by, 0.0)
    after_ref[...] = after
    before_ref[...] = before
    whole = before[SEGS - 1 :] + total[SEGS - 1 :]
    high = whole.astype(BF16)
    low = (whole - high.astype(F32)).astype(BF16)
    summary_ref[2 * NS :] = jnp.zeros((SUMMARY_ROWS - 2 * NS, width), BF16)
    summary_ref[2 * NS : 2 * NS + 1] = high
    summary_ref[2 * NS + 1 : 2 * NS + 2] = low

    def state_row(n, carry):
        state_rows, adjoint_rows = [], []
        for lane in range(0, width, 4 * LANES):
            groups = [slice(k, k + LANES) for k in range(lane, lane + 4 * LANES, LANES)]
            rate2 = [rate2_ref[n, :, cols] for cols in groups]
            state = [jnp.zeros((SEGS, LANES), F32) for _ in groups]
            adjoint = list(state)
            decays = []
            for pos in range(span):
                rows = slice(pos * SEGS, (pos + 1) * SEGS)
                b_col = b_wide[n, rows]
                decays.append([])
                for k, cols in enumerate(groups):
                    decay = jnp.exp2(rate2[k] * decay_delta[rows, cols])
                    decays[pos].append(decay)
                    state[k] = decay * state[k] + b_col * drive[rows, cols]
            for pos in reversed(range(span)):
                rows = slice(pos * SEGS, (pos + 1) * SEGS)
                c_col = c_wide[n, rows]
                for k, cols in enumerate(groups):
                    adjoint[k] = decays[pos][k] * (c_col * upstream[rows, cols] + adjoint[k])
            for k, cols in enumerate(groups):
                seg_state_ref[n, :, cols] = state[k]
                seg_adjoint_ref[n, :, cols] = adjoint[k]
                weight = jnp.exp2(rate2[k] * after_ref[:, cols])
                state_rows.append(jnp.sum(weight * state[k], axis=0, keepdims=True))
                weight = jnp.exp2(rate2[k] * before_ref[:, cols])
                adjoint_rows.append(jnp.sum(weight * adjoint[k], axis=0, keepdims=True))
        rows_ref[n] = jnp.broadcast_to(jnp.concatenate(state_rows, 1), (SEGS, width))
        rows_ref[NS + n] = jnp.broadcast_to(jnp.concatenate(adjoint_rows, 1), (SEGS, width))
        return carry

    lax.fori_loop(0, NS, state_row, 0)
    gathered = jnp.concatenate([rows_ref[n, :1] for n in range(2 * NS)], 0)
    summary_ref[: 2 * NS] = gathered.astype(BF16)


def mixer_kernel(
    own_ref, lengths_hbm, x_hbm, dt_hbm, dy_hbm, b_hbm, c_hbm, a_hbm, bias_hbm, skip_hbm,
    summaries_hbm, seg_state_hbm, seg_adjoint_hbm, seg_delta_hbm,
    out_ref, x_grad_ref, dt_grad_ref, bc_ref, params_ref,
    lengths_ref, x_ref, dt_ref, dy_ref, b_ref, c_ref, a_ref, bias_ref, skip_ref,
    summaries_ref, seg_state_ref, seg_adjoint_ref, seg_delta_ref,
    rate_ref, enter_ref, arrive_ref, b_wide, c_wide,
    delta_ref, decay_delta, drive, upstream, y_acc, xg_acc, dd_acc, bg_acc, cg_acc, rate_acc,
    semaphores,
):
    tokens, width = x_ref.shape
    span = tokens // SEGS
    count = summaries_ref.shape[0]
    own = own_ref[0]
    copies = begin_copies(
        (
            (dt_hbm.at[0], dt_ref), (bias_hbm, bias_ref), (lengths_hbm, lengths_ref),
            (a_hbm, a_ref), (summaries_hbm, summaries_ref),
            (x_hbm.at[0], x_ref), (dy_hbm.at[0], dy_ref), (skip_hbm, skip_ref),
            (b_hbm.at[0], b_ref), (c_hbm.at[0], c_ref),
            (seg_state_hbm, seg_state_ref), (seg_adjoint_hbm, seg_adjoint_ref),
            (seg_delta_hbm, seg_delta_ref),
        ),
        semaphores,
    )
    segment = to_segments(tokens).astype(BF16)
    wait_all(copies[:3])
    delta = softplus_of(dot(segment, dt_ref[...]) + bias_ref[...])
    delta_ref[...] = delta
    decay_delta[...] = with_resets(own_ref, lengths_ref, delta)
    wait_all(copies[3:])
    drive[...] = delta * dot(segment, x_ref[...])
    upstream[...] = dot(segment, dy_ref[...])
    fill_columns(segment, b_ref, c_ref, b_wide, c_wide)
    rate_all = -jnp.exp(a_ref[...])
    rate2_all = rate_all * LOG2E
    spread(rate_all, rate_ref)

    entering = jnp.zeros((NS, width), F32)
    arriving = jnp.zeros((NS, width), F32)

    def factor(j):
        ends = summaries_ref[j, 2 * NS : 2 * NS + 2].astype(F32)
        return jnp.exp2(rate2_all * (ends[0:1] + ends[1:2]))

    for j in range(count - 1):
        longer = factor(j) * entering + summaries_ref[j, :NS].astype(F32)
        entering = jnp.where(j < own, longer, entering)
    for j in reversed(range(1, count)):
        longer = factor(j) * arriving + summaries_ref[j, NS : 2 * NS].astype(F32)
        arriving = jnp.where(j > own, longer, arriving)
    spread(entering, enter_ref)
    spread(arriving, arrive_ref)

    y_acc[...] = jnp.zeros_like(y_acc)
    xg_acc[...] = jnp.zeros_like(xg_acc)
    dd_acc[...] = jnp.zeros_like(dd_acc)

    def state_row(n, carry):
        row = iota((SEGS, LANES), 0)
        for lane in range(0, width, 4 * LANES):
            groups = [slice(k, k + LANES) for k in range(lane, lane + 4 * LANES, LANES)]
            rate = [rate_ref[n, :, cols] for cols in groups]
            rate2 = [value * LOG2E for value in rate]
            state, adjoint = [], []
            for k, cols in enumerate(groups):
                seg_factor = jnp.exp2(rate2[k] * seg_delta_ref[:, cols])
                edge = enter_ref[n, :, cols]
                scale, total = seg_factor, seg_state_ref[n, :, cols]
                for by in (1, 2, 4):
                    total = total + scale * shifted(total, by, 0.0)
                    scale = scale * shifted(scale, by, 1.0)
                moved = pltpu.roll(total + scale * edge, 1, 0)
                state.append(jnp.where(row == 0, edge, moved))
                edge = arrive_ref[n, :, cols]
                scale, total = seg_factor, seg_adjoint_ref[n, :, cols]
                for by in (1, 2, 4):
                    total = total + scale * shifted(total, -by, 0.0)
                    scale = scale * shifted(scale, -by, 1.0)
                moved = pltpu.roll(total + scale * edge, SEGS - 1, 0)
                adjoint.append(jnp.where(row == SEGS - 1, edge, moved))
            decays, befores = [], []
            for pos in range(span):
                rows = slice(pos * SEGS, (pos + 1) * SEGS)
                b_col, c_col = b_wide[n, rows], c_wide[n, rows]
                decays.append([])
                befores.append(list(state))
                part = None
                for k, cols in enumerate(groups):
                    decay = jnp.exp2(rate2[k] * decay_delta[rows, cols])
                    decays[pos].append(decay)
                    state[k] = decay * state[k] + b_col * drive[rows, cols]
                    y_acc[rows, cols] += c_col * state[k]
                    term = upstream[rows, cols] * state[k]
                    part = term if part is None else part + term
                if lane == 0:
                    cg_acc[n, rows] = part
                else:
                    cg_acc[n, rows] += part
            rate_sum = [jnp.zeros((SEGS, LANES), F32) for _ in groups]
            for pos in reversed(range(span)):
                rows = slice(pos * SEGS, (pos + 1) * SEGS)
                b_col, c_col = b_wide[n, rows], c_wide[n, rows]
                part = None
                for k, cols in enumerate(groups):
                    full = c_col * upstream[rows, cols] + adjoint[k]
                    adjoint[k] = decays[pos][k] * full
                    xg_acc[rows, cols] += full * b_col
                    term = full * drive[rows, cols]
                    part = term if part is None else part + term
                    through = adjoint[k] * befores[pos][k]
                    dd_acc[rows, cols] += rate[k] * through
                    rate_sum[k] = rate_sum[k] + delta_ref[rows, cols] * through
                if lane == 0:
                    bg_acc[n, rows] = part
                else:
                    bg_acc[n, rows] += part
            for k, cols in enumerate(groups):
                rate_acc[n, :, cols] = rate[k] * rate_sum[k]
        return carry

    lax.fori_loop(0, NS, state_row, 0)

    token = to_tokens(tokens).astype(BF16)
    inputs = dot(segment, x_ref[...])
    skip = skip_ref[...]
    out_ref[...] = dot(token, (y_acc[...] + skip * inputs).astype(BF16)).astype(BF16)
    x_grad = xg_acc[...] * delta_ref[...] + skip * upstream[...]
    x_grad_ref[...] = dot(token, x_grad.astype(BF16)).astype(BF16)
    raw = dot(segment, dt_ref[...]) + bias_ref[...]
    raw_grad = (xg_acc[...] * inputs + dd_acc[...]) / (1.0 + jnp.exp(-raw))
    dt_grad_ref[...] = dot(token, raw_grad.astype(BF16)).astype(BF16)
    params_ref[:NS] = jnp.sum(rate_acc[...], axis=1)
    params_ref[NS : NS + 1] = jnp.sum(upstream[...] * inputs, axis=0, keepdims=True)
    params_ref[NS + 1 : NS + 2] = jnp.sum(raw_grad, axis=0, keepdims=True)
    lane = iota((tokens, LANES), 1)
    sums = jnp.zeros((tokens, LANES), F32)
    for k, source in enumerate((bg_acc, cg_acc)):
        for n in range(NS):
            total = jnp.sum(source[n], axis=1, keepdims=True)
            sums = jnp.where(lane == k * NS + n, total, sums)
    bc_ref[...] = exact_dot(sums.T[: 2 * NS], to_segments(tokens))


def by_head(ref):
    value = ref[...]
    return jnp.concatenate(
        [value[:, h : h + HEAD] for h in range(0, value.shape[1], HEAD)], 0
    )


def turn_back(ref, turned):
    tokens, width = ref.shape
    for h in range(width // HEAD):
        ref[:, h * HEAD : (h + 1) * HEAD] = (
            turned[:, h * tokens : (h + 1) * tokens].T.astype(ref.dtype)
        )


def key_value_copies(all_hbm, kv_ref, width):
    return [
        (all_hbm.at[:, k, :, width + v : width + v + HEAD], kv_ref.at[k, :, :, v : v + HEAD])
        for k in range(2)
        for v in (0, HEAD)
    ]


def keys_of(kv_ref, k):
    value = kv_ref[k, :, :, :HEAD]
    return value.reshape(-1, HEAD)


def values_of(kv_ref, k):
    value = kv_ref[k, :, :, HEAD:]
    return value.reshape(-1, HEAD)


def gradients(k, kv_ref, probs, query, d_att, dout_t, rowdot, kv_grad_refs):
    keys = keys_of(kv_ref, k)
    d_probs = dot(values_of(kv_ref, k), dout_t)
    d_scores = (probs * (d_probs - rowdot)).astype(BF16)
    key_grad = (dot(d_scores, query) * (HEAD ** -0.5)).astype(BF16)
    value_grad = dot(probs.astype(BF16), d_att).astype(BF16)
    tokens = kv_grad_refs[0].shape[1]
    for m in range(keys.shape[0] // tokens):
        rows = slice(m * tokens, (m + 1) * tokens)
        kv_grad_refs[m % 2][m // 2, :, :HEAD] = key_grad[rows]
        kv_grad_refs[m % 2][m // 2, :, HEAD:] = value_grad[rows]
    return dot(keys.astype(F32).T.astype(BF16), d_scores)


def inside(k, tokens, last, opening, dims):
    key = iota(dims, 0) * (2 * tokens) + iota(dims, 1) + k * tokens
    return ((key <= last) & (key >= opening)).reshape(dims[0] * dims[1], dims[2])


def attention_kernel(
    own_ref, lengths_hbm, plan_hbm, all_hbm, dout_hbm,
    out_ref, kv_near_ref, kv_far_ref, stats_ref, bounds_ref, query_ref, query_t, dout_t, query_acc,
    lengths_ref, plan_ref, picked_ref, kv_ref, dout_ref, score_ref, semaphores,
):
    tokens, width = dout_ref.shape
    columns = width // HEAD * tokens
    places = tokens // BLOCK
    half = kv_ref.shape[1] * tokens
    factor = (HEAD ** -0.5) * LOG2E
    tables = begin_copies(((plan_hbm, plan_ref), (lengths_hbm, lengths_ref)), semaphores)
    rest = begin_copies(
        [(dout_hbm.at[0], dout_ref)] + key_value_copies(all_hbm, kv_ref, width),
        semaphores.at[2:7],
    )
    wait_all(tables)
    wanted = [plan_ref[0, own_ref[0] * places + p] for p in range(places)]
    picks = []
    for p, w in enumerate(wanted):
        device, place = lax.div(w, places), lax.rem(w, places)
        rows = pl.ds(pl.multiple_of(place * BLOCK, BLOCK), BLOCK)
        picks.append((
            all_hbm.at[lax.div(device, 2), lax.rem(device, 2), rows, :width],
            picked_ref.at[p * BLOCK : (p + 1) * BLOCK],
        ))
    picks = begin_copies(picks, semaphores.at[7:])

    column = lax.rem(iota((1, columns), 1), tokens)
    place = lax.div(column, BLOCK)
    block = jnp.zeros((1, columns), jnp.int32)
    for p, w in enumerate(wanted):
        block = jnp.where(place == p, w, block)
    last = block * BLOCK + lax.rem(column, BLOCK)
    opening = jnp.zeros((1, columns), jnp.int32)
    for start in starts_of(lengths_ref):
        opening = jnp.where(start <= last, start, opening)
    bounds_ref[:1] = last
    bounds_ref[1:2] = opening

    wait_all(rest[:1])
    d_att = by_head(dout_ref)
    dout_t[...] = d_att.astype(F32).T.astype(BF16)
    wait_all(picks)
    query = by_head(picked_ref)
    query_ref[...] = query
    query_t[...] = query.astype(F32).T.astype(BF16)
    wait_all(rest[1:])

    top = jnp.full((8, columns), NEG, F32)
    for k in range(2):
        scores = dot(keys_of(kv_ref, k), query_t[...])
        dims = (half // tokens, tokens, columns)
        scores = jnp.where(inside(k, tokens, last, opening, dims), scores, NEG)
        score_ref[k] = scores
        top = jnp.maximum(top, jnp.max(scores.reshape(half // 8, 8, columns), axis=0))
    shift = jnp.max(top, axis=0, keepdims=True) * factor

    total = jnp.zeros((8, columns), F32)
    attended = jnp.zeros((HEAD, columns), F32)
    for k in range(2):
        weights = jnp.exp2(score_ref[k] * factor - shift)
        score_ref[k] = weights
        value_t = values_of(kv_ref, k).astype(F32).T.astype(BF16)
        attended = attended + dot(value_t, weights.astype(BF16))
        total = total + jnp.sum(weights.reshape(half // 8, 8, columns), axis=0)
    total = jnp.sum(total, axis=0, keepdims=True)
    inverse = 1.0 / total
    attended = (attended * inverse).astype(BF16).astype(F32)
    turn_back(out_ref, attended)
    rowdot = jnp.sum(attended * dout_t[...].astype(F32), axis=0, keepdims=True)
    stats_ref[:1] = shift + jnp.log(total) * LOG2E
    stats_ref[1:2] = rowdot

    other = 1 - lax.rem(own_ref[0], 2)
    probs = score_ref[other] * inverse
    query_acc[...] = gradients(
        other, kv_ref, probs, query, d_att, dout_t[...], rowdot, (kv_near_ref, kv_far_ref)
    )


def own_half_kernel(
    own_ref, all_hbm, dout_hbm, stats_hbm, bounds_hbm, query_hbm, query_t_hbm, dout_t_hbm, acc_hbm,
    query_grad_ref, kv_near_ref, kv_far_ref,
    kv_ref, dout_ref, stats_ref, bounds_ref, query_ref, query_t, dout_t, query_acc, semaphores,
):
    tokens, width = dout_ref.shape
    half = kv_ref.shape[1] * tokens
    columns = width // HEAD * tokens
    factor = (HEAD ** -0.5) * LOG2E
    own = lax.rem(own_ref[0], 2)
    copies = begin_copies(
        (
            (all_hbm.at[:, own, :, width : width + HEAD], kv_ref.at[0, :, :, :HEAD]),
            (query_t_hbm, query_t), (bounds_hbm, bounds_ref), (stats_hbm, stats_ref),
            (all_hbm.at[:, own, :, width + HEAD :], kv_ref.at[0, :, :, HEAD:]),
            (dout_t_hbm, dout_t), (query_hbm, query_ref), (dout_hbm.at[0], dout_ref),
            (acc_hbm, query_acc),
        ),
        semaphores,
    )
    wait_all(copies)
    scores = dot(keys_of(kv_ref, 0), query_t[...])
    dims = (half // tokens, tokens, columns)
    valid = inside(own, tokens, bounds_ref[:1], bounds_ref[1:2], dims)
    probs = jnp.where(valid, jnp.exp2(scores * factor - stats_ref[:1]), 0.0)
    part = gradients(
        0, kv_ref, probs, query_ref[...], by_head(dout_ref), dout_t[...], stats_ref[1:2],
        (kv_near_ref, kv_far_ref),
    )
    turn_back(query_grad_ref, (query_acc[...] + part) * (HEAD ** -0.5))


VMEM = pl.BlockSpec(memory_space=pltpu.VMEM)
SMEM = pl.BlockSpec(memory_space=pltpu.SMEM)
HBM = pl.BlockSpec(memory_space=pltpu.HBM)
PARAMS = pltpu.CompilerParams(vmem_limit_bytes=63 * 1024 * 1024)


def shape(*dims, dtype=F32):
    return jax.ShapeDtypeStruct(dims, dtype)


def wide(*dims, dtype=F32):
    return pltpu.VMEM(dims, dtype)


def run_summary(own, lengths, x, dt, dy, b, c, a_log, bias):
    tokens, width = x.shape[1:]
    return pl.pallas_call(
        summary_kernel,
        out_shape=(
            shape(SUMMARY_ROWS, width, dtype=BF16),
            shape(NS, SEGS, width), shape(NS, SEGS, width), shape(SEGS, width),
        ),
        in_specs=[SMEM] + [HBM] * 8,
        out_specs=[VMEM] * 4,
        scratch_shapes=[
            pltpu.SMEM(lengths.shape, jnp.int32),
            wide(tokens, width, dtype=BF16), wide(tokens, width, dtype=BF16),
            wide(tokens, width, dtype=BF16),
            wide(NS, tokens, dtype=BF16), wide(NS, tokens, dtype=BF16),
            wide(NS, width), wide(1, width),
            wide(NS, SEGS, width), wide(NS, tokens, LANES), wide(NS, tokens, LANES),
            wide(tokens, width), wide(tokens, width), wide(tokens, width),
            wide(SEGS, width), wide(SEGS, width), wide(2 * NS, SEGS, width),
            pltpu.SemaphoreType.DMA((8,)),
        ],
        compiler_params=PARAMS,
        name="mixer_summary",
    )(own, lengths, x, dt, dy, b, c, a_log, bias)


def run_mixer(own, lengths, x, dt, dy, b, c, a_log, bias, skip, summaries, local):
    tokens, width = x.shape[1:]
    return pl.pallas_call(
        mixer_kernel,
        out_shape=(
            shape(tokens, width, dtype=BF16), shape(tokens, width, dtype=BF16),
            shape(tokens, width, dtype=BF16), shape(2 * NS, tokens), shape(NS + 2, width),
        ),
        in_specs=[SMEM] + [HBM] * 13,
        out_specs=[VMEM] * 5,
        scratch_shapes=[
            pltpu.SMEM(lengths.shape, jnp.int32),
            wide(tokens, width, dtype=BF16), wide(tokens, width, dtype=BF16),
            wide(tokens, width, dtype=BF16),
            wide(NS, tokens, dtype=BF16), wide(NS, tokens, dtype=BF16),
            wide(NS, width), wide(1, width), wide(1, width),
            wide(*summaries.shape, dtype=BF16),
            wide(NS, SEGS, width), wide(NS, SEGS, width), wide(SEGS, width),
            wide(NS, SEGS, width), wide(NS, SEGS, width), wide(NS, SEGS, width),
            wide(NS, tokens, LANES), wide(NS, tokens, LANES),
            wide(tokens, width), wide(tokens, width), wide(tokens, width), wide(tokens, width),
            wide(tokens, width), wide(tokens, width), wide(tokens, width),
            wide(NS, tokens, LANES), wide(NS, tokens, LANES),
            wide(NS, SEGS, width),
            pltpu.SemaphoreType.DMA((13,)),
        ],
        compiler_params=PARAMS,
        name="mixer",
    )(own, lengths, x, dt, dy, b, c, a_log, bias, skip, summaries, *local)


def run_attention(own, lengths, plan, gathered, dout):
    tokens, width = dout.shape[1:]
    pairs = gathered.shape[0]
    columns = width // HEAD * tokens
    kv_shape = shape(pairs // 2, tokens, 2 * HEAD, dtype=BF16)
    out, near, far, *carried = pl.pallas_call(
        attention_kernel,
        out_shape=(
            shape(tokens, width, dtype=BF16), kv_shape, kv_shape,
            shape(8, columns), shape(8, columns, dtype=jnp.int32),
            shape(columns, HEAD, dtype=BF16), shape(HEAD, columns, dtype=BF16),
            shape(HEAD, columns, dtype=BF16), shape(HEAD, columns),
        ),
        in_specs=[SMEM] + [HBM] * 4,
        out_specs=[VMEM] * 9,
        scratch_shapes=[
            pltpu.SMEM(lengths.shape, jnp.int32), pltpu.SMEM(plan.shape, jnp.int32),
            wide(tokens, width, dtype=BF16), wide(2, pairs, tokens, 2 * HEAD, dtype=BF16),
            wide(tokens, width, dtype=BF16), wide(2, pairs * tokens, columns),
            pltpu.SemaphoreType.DMA((7 + tokens // BLOCK,)),
        ],
        compiler_params=PARAMS,
        name="attention",
    )(own, lengths, plan, gathered, dout)
    return out, (near, far), carried


def run_own_half(own, gathered, dout, carried):
    tokens, width = dout.shape[1:]
    pairs = gathered.shape[0]
    columns = width // HEAD * tokens
    kv_shape = shape(pairs // 2, tokens, 2 * HEAD, dtype=BF16)
    query_grad, *kv_parts = pl.pallas_call(
        own_half_kernel,
        out_shape=(shape(tokens, width, dtype=BF16), kv_shape, kv_shape),
        in_specs=[SMEM] + [HBM] * 8,
        out_specs=[VMEM] * 3,
        scratch_shapes=[
            wide(1, pairs, tokens, 2 * HEAD, dtype=BF16), wide(tokens, width, dtype=BF16),
            wide(8, columns), wide(8, columns, dtype=jnp.int32),
            wide(columns, HEAD, dtype=BF16), wide(HEAD, columns, dtype=BF16),
            wide(HEAD, columns, dtype=BF16), wide(HEAD, columns),
            pltpu.SemaphoreType.DMA((9,)),
        ],
        compiler_params=PARAMS,
        name="attention_own_half",
    )(own, gathered, dout, *carried)
    return query_grad, kv_parts


def on_device(
    x_in, dt_in, b_in, c_in, dy_in, a_log, d_skip, dt_bias,
    q_in, k_in, value_input, dout_in, doc_lengths, plan,
):
    seq_count = lax.axis_size("seq")
    own = lax.axis_index("seq").astype(jnp.int32).reshape(1)
    tokens = x_in.shape[1]
    mixer_inputs = (
        own, doc_lengths, x_in, dt_in, dy_in, b_in, c_in, a_log, dt_bias[None],
    )

    mixed = jnp.concatenate([q_in[0], k_in[0], value_input[0]], axis=1)
    gathered = lax.all_gather(mixed, "seq", axis=0, tiled=True)

    summary, *local = run_summary(*mixer_inputs)
    summaries = lax.all_gather(summary, "seq", axis=0)
    output, x_grad, dt_grad, bc_part, params = run_mixer(
        *mixer_inputs, d_skip[None], summaries, local
    )
    one_side = [(i, i ^ 1) for i in range(seq_count)]
    other_side = [(i, (((i + 1) ^ 1) - 1) % seq_count) for i in range(seq_count)]
    same_parity = [
        [*range(k, seq_count, 4), *range(k + 2, seq_count, 4)] for k in range(2)
    ]
    params = params + lax.ppermute(params, "seq", one_side)
    params = jnp.sum(lax.all_gather(params, "dp", axis=0), axis=0)
    gathered, params = lax.optimization_barrier((gathered, params))

    gathered = gathered.reshape(seq_count // 2, 2, tokens, -1)
    attn_out, kv_other, carried = run_attention(own, doc_lengths, plan, gathered, dout_in)
    arrived = [
        lax.ppermute(part, "seq", pairs) for part, pairs in zip(kv_other, (one_side, other_side))
    ]
    query_gradient, kv_own = run_own_half(own, gathered, dout_in, carried)
    kv_pair = [(a.astype(F32) + b.astype(F32)).astype(BF16) for a, b in zip(kv_own, arrived)]
    split = jnp.concatenate([params[:, : 2 * HEAD], params[:, 2 * HEAD :]], 0).astype(BF16)
    spare = -split.shape[0] % 8
    split = jnp.pad(split, ((0, spare), (0, 0)))
    split = jnp.broadcast_to(split[None], (seq_count // 2, *split.shape))
    sent = jnp.concatenate([jnp.concatenate(kv_pair, 0), split], 1)
    sent, bc_part = lax.optimization_barrier((sent, bc_part))
    parts = lax.all_to_all(
        sent, "seq", split_axis=0, concat_axis=0, axis_index_groups=same_parity
    )
    bc_sum = jnp.sum(lax.all_gather(bc_part, "tp", axis=0), axis=0)
    sums = jnp.sum(parts.astype(F32), axis=0)
    kv_sum = sums[:tokens].astype(BF16)
    rows = params.shape[0]
    params_sum = jnp.concatenate(
        [sums[tokens : tokens + rows], sums[tokens + rows : tokens + 2 * rows]], 1
    )
    return (
        output[None],
        x_grad[None],
        dt_grad[None],
        bc_sum[None, :NS],
        bc_sum[None, NS:],
        params_sum[:NS],
        params_sum[NS],
        params_sum[NS + 1],
        attn_out[None],
        query_gradient[None],
        kv_sum[None, :, :HEAD],
        kv_sum[None, :, HEAD:],
    )


def solution(mesh):
    tokens = P("dp", "seq", "tp")
    columns = P("dp", None, "seq")
    row = P("dp", None)
    return jax.shard_map(
        on_device,
        mesh=mesh,
        in_specs=(
            tokens, tokens, columns, columns, tokens, P(None, "tp"), P("tp"), P("tp"),
            tokens, tokens, tokens, tokens, row, row,
        ),
        out_specs=(
            tokens, tokens, tokens, columns, columns, P(None, "tp"), P("tp"), P("tp"),
            tokens, tokens, tokens, tokens,
        ),
        check_vma=False,
    )
```

```python
import jax
import jax.numpy as jnp
from jax import lax
from jax.experimental import pallas as pl
from jax.experimental.pallas import tpu as pltpu
from jax.sharding import PartitionSpec as P

NS = 16
HEAD = 128
BLOCK = 32
LANES = 128
SEGS = 8
RESET = 1e30
LOG2E = 1.4426950408889634
NEG = -1e30

F32 = jnp.float32
BF16 = jnp.bfloat16


def dot(a, b, dims=((1,), (0,)), precision=None):
    return lax.dot_general(a, b, (dims, ((), ())), precision=precision, preferred_element_type=F32)


def exact_dot(a, b, dims=((1,), (0,))):
    return dot(a, b, dims, lax.Precision.HIGHEST)


def iota(shape, axis):
    return lax.broadcasted_iota(jnp.int32, shape, axis)


def to_segments(tokens):
    span = tokens // SEGS
    row = iota((tokens, tokens), 0)
    token = iota((tokens, tokens), 1)
    return jnp.where(token == lax.rem(row, SEGS) * span + lax.div(row, SEGS), 1.0, 0.0)


def to_tokens(tokens):
    span = tokens // SEGS
    token = iota((tokens, tokens), 0)
    row = iota((tokens, tokens), 1)
    return jnp.where(row == lax.rem(token, span) * SEGS + lax.div(token, span), 1.0, 0.0)


def starts_of(lengths_ref):
    starts = [jnp.int32(0)]
    for k in range(lengths_ref.shape[1] - 1):
        starts.append(starts[-1] + lengths_ref[0, k])
    return starts


def begin_copies(pairs, semaphores):
    copies = [
        pltpu.make_async_copy(source, target, semaphores.at[k])
        for k, (source, target) in enumerate(pairs)
    ]
    for copy in copies:
        copy.start()
    return copies


def wait_all(copies):
    for copy in copies:
        copy.wait()


def softplus_of(raw):
    small = jnp.exp(-jnp.abs(raw))
    one = 1.0 + small
    tail = one - 1.0
    safe = jnp.where(tail == 0.0, 1.0, tail)
    log1p = jnp.where(tail == 0.0, small, jnp.log(one) * (small / safe))
    return jnp.maximum(raw, 0.0) + log1p


def with_resets(own_ref, lengths_ref, delta):
    tokens = delta.shape[0]
    span = tokens // SEGS
    row = iota(delta.shape, 0)
    token = own_ref[0] * tokens + lax.rem(row, SEGS) * span + lax.div(row, SEGS)
    first = token == 0
    for start in starts_of(lengths_ref):
        first = first | (token == start)
    return jnp.where(first, RESET, delta)


def spread(source, target):
    for n in range(NS):
        target[n] = jnp.broadcast_to(source[n : n + 1], target.shape[1:])


def fill_columns(segment, b_ref, c_ref, b_wide, c_wide):
    tokens = segment.shape[0]
    for source, target in ((b_ref, b_wide), (c_ref, c_wide)):
        columns = dot(segment, source[...], ((1,), (1,)))
        for n in range(NS):
            target[n] = jnp.broadcast_to(columns[:, n : n + 1], (tokens, LANES))


def shifted(value, by, fill):
    rows = value.shape[0]
    row = iota(value.shape, 0)
    moved = pltpu.roll(value, by % rows, 0)
    return jnp.where((row >= by) & (row < rows + by), moved, fill)


def summary_kernel(
    own_ref, lengths_hbm, x_hbm, dt_hbm, dy_hbm, b_hbm, c_hbm, a_hbm, bias_hbm,
    summary_ref, seg_state_ref, seg_adjoint_ref, seg_delta_ref,
    lengths_ref, x_ref, dt_ref, dy_ref, b_ref, c_ref, a_ref, bias_ref,
    rate2_ref, b_wide, c_wide, decay_delta, drive, upstream, before_ref, after_ref, rows_ref, semaphores,
):
    tokens, width = x_ref.shape
    span = tokens // SEGS
    copies = begin_copies(
        (
            (dt_hbm.at[0], dt_ref), (bias_hbm, bias_ref), (lengths_hbm, lengths_ref),
            (x_hbm.at[0], x_ref), (dy_hbm.at[0], dy_ref), (a_hbm, a_ref),
            (b_hbm.at[0], b_ref), (c_hbm.at[0], c_ref),
        ),
        semaphores,
    )
    segment = to_segments(tokens).astype(BF16)
    wait_all(copies[:3])
    raw = dot(segment, dt_ref[...]) + bias_ref[...]
    delta = softplus_of(raw)
    reset_delta = with_resets(own_ref, lengths_ref, delta)
    decay_delta[...] = reset_delta
    wait_all(copies[3:])
    drive[...] = delta * dot(segment, x_ref[...])
    upstream[...] = dot(segment, dy_ref[...])
    spread(-jnp.exp(a_ref[...]) * LOG2E, rate2_ref)
    fill_columns(segment, b_ref, c_ref, b_wide, c_wide)

    total = reset_delta[:SEGS]
    for pos in range(1, span):
        total = total + reset_delta[pos * SEGS : (pos + 1) * SEGS]
    seg_delta_ref[...] = total
    after = shifted(total, -1, 0.0)
    before = shifted(total, 1, 0.0)
    for by in (1, 2, 4):
        after = after + shifted(after, -by, 0.0)
        before = before + shifted(before, by, 0.0)
    after_ref[...] = after
    before_ref[...] = before
    whole = before[SEGS - 1 :] + total[SEGS - 1 :]
    high = whole.astype(BF16).astype(F32)
    low = whole - high
    ends = [part[:, lane : lane + LANES] for part in (high, low) for lane in range(0, width, LANES)]
    summary_ref[2 * NS * width // LANES :] = jnp.concatenate(ends, 0).astype(BF16)

    def state_row(n, carry):
        state_rows, adjoint_rows = [], []
        for lane in range(0, width, 4 * LANES):
            groups = [slice(k, k + LANES) for k in range(lane, lane + 4 * LANES, LANES)]
            rate2 = [rate2_ref[n, :, cols] for cols in groups]
            state = [jnp.zeros((SEGS, LANES), F32) for _ in groups]
            adjoint = list(state)
            decays = []
            for pos in range(span):
                rows = slice(pos * SEGS, (pos + 1) * SEGS)
                b_col = b_wide[n, rows]
                decays.append([])
                for k, cols in enumerate(groups):
                    decay = jnp.exp2(rate2[k] * decay_delta[rows, cols])
                    decays[pos].append(decay)
                    state[k] = decay * state[k] + b_col * drive[rows, cols]
            for pos in reversed(range(span)):
                rows = slice(pos * SEGS, (pos + 1) * SEGS)
                c_col = c_wide[n, rows]
                for k, cols in enumerate(groups):
                    adjoint[k] = decays[pos][k] * (c_col * upstream[rows, cols] + adjoint[k])
            for k, cols in enumerate(groups):
                seg_state_ref[n, :, cols] = state[k]
                seg_adjoint_ref[n, :, cols] = adjoint[k]
                weight = jnp.exp2(rate2[k] * after_ref[:, cols])
                state_rows.append(jnp.sum(weight * state[k], axis=0, keepdims=True))
                weight = jnp.exp2(rate2[k] * before_ref[:, cols])
                adjoint_rows.append(jnp.sum(weight * adjoint[k], axis=0, keepdims=True))
        rows_ref[n] = jnp.broadcast_to(jnp.concatenate(state_rows, 1), (SEGS, width))
        rows_ref[NS + n] = jnp.broadcast_to(jnp.concatenate(adjoint_rows, 1), (SEGS, width))
        return carry

    lax.fori_loop(0, NS, state_row, 0)
    gathered = jnp.concatenate([rows_ref[n, :1] for n in range(2 * NS)], 0)
    for k in range(width // LANES):
        rows = slice(2 * NS * k, 2 * NS * (k + 1))
        summary_ref[rows] = gathered[:, k * LANES : (k + 1) * LANES].astype(BF16)


def mixer_kernel(
    own_ref, lengths_hbm, x_hbm, dt_hbm, dy_hbm, b_hbm, c_hbm, a_hbm, bias_hbm, skip_hbm,
    summaries_hbm, seg_state_hbm, seg_adjoint_hbm, seg_delta_hbm,
    out_ref, x_grad_ref, dt_grad_ref, bc_ref, params_ref,
    lengths_ref, x_ref, dt_ref, dy_ref, b_ref, c_ref, a_ref, bias_ref, skip_ref,
    summaries_ref, seg_state_ref, seg_adjoint_ref, seg_delta_ref,
    rate_ref, enter_ref, arrive_ref, b_wide, c_wide,
    delta_ref, decay_delta, drive, upstream, y_acc, xg_acc, dd_acc, bg_acc, cg_acc, rate_acc,
    semaphores,
):
    tokens, width = x_ref.shape
    span = tokens // SEGS
    count = summaries_ref.shape[0]
    own = own_ref[0]
    copies = begin_copies(
        (
            (dt_hbm.at[0], dt_ref), (bias_hbm, bias_ref), (lengths_hbm, lengths_ref),
            (a_hbm, a_ref), (summaries_hbm, summaries_ref),
            (x_hbm.at[0], x_ref), (dy_hbm.at[0], dy_ref), (skip_hbm, skip_ref),
            (b_hbm.at[0], b_ref), (c_hbm.at[0], c_ref),
            (seg_state_hbm, seg_state_ref), (seg_adjoint_hbm, seg_adjoint_ref),
            (seg_delta_hbm, seg_delta_ref),
        ),
        semaphores,
    )
    segment = to_segments(tokens).astype(BF16)
    wait_all(copies[:3])
    delta = softplus_of(dot(segment, dt_ref[...]) + bias_ref[...])
    delta_ref[...] = delta
    decay_delta[...] = with_resets(own_ref, lengths_ref, delta)
    wait_all(copies[3:])
    drive[...] = delta * dot(segment, x_ref[...])
    upstream[...] = dot(segment, dy_ref[...])
    fill_columns(segment, b_ref, c_ref, b_wide, c_wide)
    rate_all = -jnp.exp(a_ref[...])
    rate2_all = rate_all * LOG2E
    spread(rate_all, rate_ref)

    entering = jnp.zeros((NS, width), F32)
    arriving = jnp.zeros((NS, width), F32)

    groups = width // LANES

    def factor(j):
        ends = summaries_ref[j, 2 * NS * groups :].astype(F32)
        ends = ends[:groups] + ends[groups:]
        return jnp.exp2(rate2_all * jnp.concatenate([ends[k : k + 1] for k in range(groups)], 1))

    def summed(j, first):
        starts = range(first, 2 * NS * groups, 2 * NS)
        return jnp.concatenate([summaries_ref[j, k : k + NS].astype(F32) for k in starts], 1)

    for j in range(count - 1):
        longer = factor(j) * entering + summed(j, 0)
        entering = jnp.where(j < own, longer, entering)
    for j in reversed(range(1, count)):
        longer = factor(j) * arriving + summed(j, NS)
        arriving = jnp.where(j > own, longer, arriving)
    spread(entering, enter_ref)
    spread(arriving, arrive_ref)

    y_acc[...] = jnp.zeros_like(y_acc)
    xg_acc[...] = jnp.zeros_like(xg_acc)
    dd_acc[...] = jnp.zeros_like(dd_acc)

    def state_row(n, carry):
        row = iota((SEGS, LANES), 0)
        for lane in range(0, width, 4 * LANES):
            groups = [slice(k, k + LANES) for k in range(lane, lane + 4 * LANES, LANES)]
            rate = [rate_ref[n, :, cols] for cols in groups]
            rate2 = [value * LOG2E for value in rate]
            state, adjoint = [], []
            for k, cols in enumerate(groups):
                seg_factor = jnp.exp2(rate2[k] * seg_delta_ref[:, cols])
                edge = enter_ref[n, :, cols]
                scale, total = seg_factor, seg_state_ref[n, :, cols]
                for by in (1, 2, 4):
                    total = total + scale * shifted(total, by, 0.0)
                    scale = scale * shifted(scale, by, 1.0)
                moved = pltpu.roll(total + scale * edge, 1, 0)
                state.append(jnp.where(row == 0, edge, moved))
                edge = arrive_ref[n, :, cols]
                scale, total = seg_factor, seg_adjoint_ref[n, :, cols]
                for by in (1, 2, 4):
                    total = total + scale * shifted(total, -by, 0.0)
                    scale = scale * shifted(scale, -by, 1.0)
                moved = pltpu.roll(total + scale * edge, SEGS - 1, 0)
                adjoint.append(jnp.where(row == SEGS - 1, edge, moved))
            decays, befores = [], []
            for pos in range(span):
                rows = slice(pos * SEGS, (pos + 1) * SEGS)
                b_col, c_col = b_wide[n, rows], c_wide[n, rows]
                decays.append([])
                befores.append(list(state))
                part = None
                for k, cols in enumerate(groups):
                    decay = jnp.exp2(rate2[k] * decay_delta[rows, cols])
                    decays[pos].append(decay)
                    state[k] = decay * state[k] + b_col * drive[rows, cols]
                    y_acc[rows, cols] += c_col * state[k]
                    term = upstream[rows, cols] * state[k]
                    part = term if part is None else part + term
                if lane == 0:
                    cg_acc[n, rows] = part
                else:
                    cg_acc[n, rows] += part
            rate_sum = [jnp.zeros((SEGS, LANES), F32) for _ in groups]
            for pos in reversed(range(span)):
                rows = slice(pos * SEGS, (pos + 1) * SEGS)
                b_col, c_col = b_wide[n, rows], c_wide[n, rows]
                part = None
                for k, cols in enumerate(groups):
                    full = c_col * upstream[rows, cols] + adjoint[k]
                    adjoint[k] = decays[pos][k] * full
                    xg_acc[rows, cols] += full * b_col
                    term = full * drive[rows, cols]
                    part = term if part is None else part + term
                    through = adjoint[k] * befores[pos][k]
                    dd_acc[rows, cols] += rate[k] * through
                    rate_sum[k] = rate_sum[k] + delta_ref[rows, cols] * through
                if lane == 0:
                    bg_acc[n, rows] = part
                else:
                    bg_acc[n, rows] += part
            for k, cols in enumerate(groups):
                rate_acc[n, :, cols] = rate[k] * rate_sum[k]
        return carry

    lax.fori_loop(0, NS, state_row, 0)

    token = to_tokens(tokens).astype(BF16)
    inputs = dot(segment, x_ref[...])
    skip = skip_ref[...]
    out_ref[...] = dot(token, (y_acc[...] + skip * inputs).astype(BF16)).astype(BF16)
    x_grad = xg_acc[...] * delta_ref[...] + skip * upstream[...]
    x_grad_ref[...] = dot(token, x_grad.astype(BF16)).astype(BF16)
    raw = dot(segment, dt_ref[...]) + bias_ref[...]
    raw_grad = (xg_acc[...] * inputs + dd_acc[...]) / (1.0 + jnp.exp(-raw))
    dt_grad_ref[...] = dot(token, raw_grad.astype(BF16)).astype(BF16)
    params_ref[:NS] = jnp.sum(rate_acc[...], axis=1)
    params_ref[NS : NS + 1] = jnp.sum(upstream[...] * inputs, axis=0, keepdims=True)
    params_ref[NS + 1 : NS + 2] = jnp.sum(raw_grad, axis=0, keepdims=True)
    lane = iota((tokens, LANES), 1)
    sums = jnp.zeros((tokens, LANES), F32)
    for k, source in enumerate((bg_acc, cg_acc)):
        for n in range(NS):
            total = jnp.sum(source[n], axis=1, keepdims=True)
            sums = jnp.where(lane == k * NS + n, total, sums)
    bc_ref[...] = exact_dot(sums.T[: 2 * NS], to_segments(tokens))


def by_head(ref):
    value = ref[...]
    return jnp.concatenate(
        [value[:, h : h + HEAD] for h in range(0, value.shape[1], HEAD)], 0
    )


def turn_back(ref, turned):
    tokens, width = ref.shape
    for h in range(width // HEAD):
        ref[:, h * HEAD : (h + 1) * HEAD] = (
            turned[:, h * tokens : (h + 1) * tokens].T.astype(ref.dtype)
        )


def key_value_copies(all_hbm, kv_ref, width):
    return [
        (all_hbm.at[:, k, :, width + v : width + v + HEAD], kv_ref.at[k, :, :, v : v + HEAD])
        for k in range(2)
        for v in (0, HEAD)
    ]


def keys_of(kv_ref, k):
    value = kv_ref[k, :, :, :HEAD]
    return value.reshape(-1, HEAD)


def values_of(kv_ref, k):
    value = kv_ref[k, :, :, HEAD:]
    return value.reshape(-1, HEAD)


def gradients(k, kv_ref, probs, query, d_att, dout_t, rowdot, kv_grad_refs):
    keys = keys_of(kv_ref, k)
    d_probs = dot(values_of(kv_ref, k), dout_t)
    d_scores = (probs * (d_probs - rowdot)).astype(BF16)
    key_grad = (dot(d_scores, query) * (HEAD ** -0.5)).astype(BF16)
    value_grad = dot(probs.astype(BF16), d_att).astype(BF16)
    tokens = kv_grad_refs[0].shape[1]
    for m in range(keys.shape[0] // tokens):
        rows = slice(m * tokens, (m + 1) * tokens)
        kv_grad_refs[m % 2][m // 2, :, :HEAD] = key_grad[rows]
        kv_grad_refs[m % 2][m // 2, :, HEAD:] = value_grad[rows]
    return dot(keys.astype(F32).T.astype(BF16), d_scores)


def inside(k, tokens, last, opening, dims):
    key = iota(dims, 0) * (2 * tokens) + iota(dims, 1) + k * tokens
    return ((key <= last) & (key >= opening)).reshape(dims[0] * dims[1], dims[2])


def attention_kernel(
    own_ref, lengths_ref, plan_ref, all_hbm, dout_hbm,
    out_ref, kv_near_ref, kv_far_ref, stats_ref, bounds_ref, query_ref, query_t, dout_t, query_acc,
    picked_ref, kv_ref, dout_ref, score_ref, semaphores,
):
    tokens, width = dout_ref.shape
    columns = width // HEAD * tokens
    places = tokens // BLOCK
    half = kv_ref.shape[1] * tokens
    factor = (HEAD ** -0.5) * LOG2E
    wanted = [plan_ref[0, own_ref[0] * places + p] for p in range(places)]
    picks = []
    for p, w in enumerate(wanted):
        device, place = lax.div(w, places), lax.rem(w, places)
        rows = pl.ds(pl.multiple_of(place * BLOCK, BLOCK), BLOCK)
        picks.append((
            all_hbm.at[lax.div(device, 2), lax.rem(device, 2), rows, :width],
            picked_ref.at[p * BLOCK : (p + 1) * BLOCK],
        ))
    picks = begin_copies(picks, semaphores.at[5:])
    rest = begin_copies(
        [(dout_hbm.at[0], dout_ref)] + key_value_copies(all_hbm, kv_ref, width), semaphores
    )

    column = lax.rem(iota((1, columns), 1), tokens)
    place = lax.div(column, BLOCK)
    block = jnp.zeros((1, columns), jnp.int32)
    for p, w in enumerate(wanted):
        block = jnp.where(place == p, w, block)
    last = block * BLOCK + lax.rem(column, BLOCK)
    opening = jnp.zeros((1, columns), jnp.int32)
    for start in starts_of(lengths_ref):
        opening = jnp.where(start <= last, start, opening)
    bounds_ref[:1] = last
    bounds_ref[1:2] = opening

    wait_all(rest[:1])
    d_att = by_head(dout_ref)
    dout_t[...] = d_att.astype(F32).T.astype(BF16)
    wait_all(picks)
    query = by_head(picked_ref)
    query_ref[...] = query
    query_t[...] = query.astype(F32).T.astype(BF16)
    wait_all(rest[1:])

    top = jnp.full((8, columns), NEG, F32)
    for k in range(2):
        scores = dot(keys_of(kv_ref, k), query_t[...])
        dims = (half // tokens, tokens, columns)
        scores = jnp.where(inside(k, tokens, last, opening, dims), scores, NEG)
        score_ref[k] = scores
        top = jnp.maximum(top, jnp.max(scores.reshape(half // 8, 8, columns), axis=0))
    shift = jnp.max(top, axis=0, keepdims=True) * factor

    total = jnp.zeros((8, columns), F32)
    attended = jnp.zeros((HEAD, columns), F32)
    other = 1 - lax.rem(own_ref[0], 2)
    for k in (1 - other, other):
        weights = jnp.exp2(score_ref[k] * factor - shift)
        value_t = values_of(kv_ref, k).astype(F32).T.astype(BF16)
        attended = attended + dot(value_t, weights.astype(BF16))
        total = total + jnp.sum(weights.reshape(half // 8, 8, columns), axis=0)
    total = jnp.sum(total, axis=0, keepdims=True)
    inverse = 1.0 / total
    attended = (attended * inverse).astype(BF16).astype(F32)
    turn_back(out_ref, attended)
    rowdot = jnp.sum(attended * dout_t[...].astype(F32), axis=0, keepdims=True)
    stats_ref[:1] = shift + jnp.log(total) * LOG2E
    stats_ref[1:2] = rowdot

    probs = weights * inverse
    query_acc[...] = gradients(
        other, kv_ref, probs, query, d_att, dout_t[...], rowdot, (kv_near_ref, kv_far_ref)
    )


def own_half_kernel(
    own_ref, all_hbm, dout_hbm, stats_hbm, bounds_hbm, query_hbm, query_t_hbm, dout_t_hbm, acc_hbm,
    query_grad_ref, kv_near_ref, kv_far_ref,
    kv_ref, dout_ref, stats_ref, bounds_ref, query_ref, query_t, dout_t, query_acc, semaphores,
):
    tokens, width = dout_ref.shape
    half = kv_ref.shape[1] * tokens
    columns = width // HEAD * tokens
    factor = (HEAD ** -0.5) * LOG2E
    own = lax.rem(own_ref[0], 2)
    copies = begin_copies(
        (
            (all_hbm.at[:, own, :, width : width + HEAD], kv_ref.at[0, :, :, :HEAD]),
            (query_t_hbm, query_t), (bounds_hbm, bounds_ref), (stats_hbm, stats_ref),
            (all_hbm.at[:, own, :, width + HEAD :], kv_ref.at[0, :, :, HEAD:]),
            (dout_t_hbm, dout_t), (query_hbm, query_ref), (dout_hbm.at[0], dout_ref),
            (acc_hbm, query_acc),
        ),
        semaphores,
    )
    wait_all(copies[:4])
    scores = dot(keys_of(kv_ref, 0), query_t[...])
    dims = (half // tokens, tokens, columns)
    valid = inside(own, tokens, bounds_ref[:1], bounds_ref[1:2], dims)
    probs = jnp.where(valid, jnp.exp2(scores * factor - stats_ref[:1]), 0.0)
    wait_all(copies[4:])
    part = gradients(
        0, kv_ref, probs, query_ref[...], by_head(dout_ref), dout_t[...], stats_ref[1:2],
        (kv_near_ref, kv_far_ref),
    )
    turn_back(query_grad_ref, (query_acc[...] + part) * (HEAD ** -0.5))


VMEM = pl.BlockSpec(memory_space=pltpu.VMEM)
SMEM = pl.BlockSpec(memory_space=pltpu.SMEM)
HBM = pl.BlockSpec(memory_space=pltpu.HBM)
PARAMS = pltpu.CompilerParams(vmem_limit_bytes=63 * 1024 * 1024)


def shape(*dims, dtype=F32):
    return jax.ShapeDtypeStruct(dims, dtype)


def wide(*dims, dtype=F32):
    return pltpu.VMEM(dims, dtype)


def run_summary(own, lengths, x, dt, dy, b, c, a_log, bias):
    tokens, width = x.shape[1:]
    return pl.pallas_call(
        summary_kernel,
        out_shape=(
            shape(2 * (NS + 1) * width // LANES, LANES, dtype=BF16),
            shape(NS, SEGS, width), shape(NS, SEGS, width), shape(SEGS, width),
        ),
        in_specs=[SMEM] + [HBM] * 8,
        out_specs=[VMEM] * 4,
        scratch_shapes=[
            pltpu.SMEM(lengths.shape, jnp.int32),
            wide(tokens, width, dtype=BF16), wide(tokens, width, dtype=BF16),
            wide(tokens, width, dtype=BF16),
            wide(NS, tokens, dtype=BF16), wide(NS, tokens, dtype=BF16),
            wide(NS, width), wide(1, width),
            wide(NS, SEGS, width), wide(NS, tokens, LANES), wide(NS, tokens, LANES),
            wide(tokens, width), wide(tokens, width), wide(tokens, width),
            wide(SEGS, width), wide(SEGS, width), wide(2 * NS, SEGS, width),
            pltpu.SemaphoreType.DMA((8,)),
        ],
        compiler_params=PARAMS,
        name="mixer_summary",
    )(own, lengths, x, dt, dy, b, c, a_log, bias)


def run_mixer(own, lengths, x, dt, dy, b, c, a_log, bias, skip, summaries, local):
    tokens, width = x.shape[1:]
    return pl.pallas_call(
        mixer_kernel,
        out_shape=(
            shape(tokens, width, dtype=BF16), shape(tokens, width, dtype=BF16),
            shape(tokens, width, dtype=BF16), shape(2 * NS, tokens), shape(NS + 2, width),
        ),
        in_specs=[SMEM] + [HBM] * 13,
        out_specs=[VMEM] * 5,
        scratch_shapes=[
            pltpu.SMEM(lengths.shape, jnp.int32),
            wide(tokens, width, dtype=BF16), wide(tokens, width, dtype=BF16),
            wide(tokens, width, dtype=BF16),
            wide(NS, tokens, dtype=BF16), wide(NS, tokens, dtype=BF16),
            wide(NS, width), wide(1, width), wide(1, width),
            wide(*summaries.shape, dtype=BF16),
            wide(NS, SEGS, width), wide(NS, SEGS, width), wide(SEGS, width),
            wide(NS, SEGS, width), wide(NS, SEGS, width), wide(NS, SEGS, width),
            wide(NS, tokens, LANES), wide(NS, tokens, LANES),
            wide(tokens, width), wide(tokens, width), wide(tokens, width), wide(tokens, width),
            wide(tokens, width), wide(tokens, width), wide(tokens, width),
            wide(NS, tokens, LANES), wide(NS, tokens, LANES),
            wide(NS, SEGS, width),
            pltpu.SemaphoreType.DMA((13,)),
        ],
        compiler_params=PARAMS,
        name="mixer",
    )(own, lengths, x, dt, dy, b, c, a_log, bias, skip, summaries, *local)


def run_attention(own, lengths, plan, gathered, dout):
    tokens, width = dout.shape[1:]
    pairs = gathered.shape[0]
    columns = width // HEAD * tokens
    kv_shape = shape(pairs // 2, tokens, 2 * HEAD, dtype=BF16)
    out, near, far, *carried = pl.pallas_call(
        attention_kernel,
        out_shape=(
            shape(tokens, width, dtype=BF16), kv_shape, kv_shape,
            shape(8, columns), shape(8, columns, dtype=jnp.int32),
            shape(columns, HEAD, dtype=BF16), shape(HEAD, columns, dtype=BF16),
            shape(HEAD, columns, dtype=BF16), shape(HEAD, columns),
        ),
        in_specs=[SMEM] * 3 + [HBM] * 2,
        out_specs=[VMEM] * 9,
        scratch_shapes=[
            wide(tokens, width, dtype=BF16), wide(2, pairs, tokens, 2 * HEAD, dtype=BF16),
            wide(tokens, width, dtype=BF16), wide(2, pairs * tokens, columns),
            pltpu.SemaphoreType.DMA((5 + tokens // BLOCK,)),
        ],
        compiler_params=PARAMS,
        cost_estimate=pl.CostEstimate(
            flops=10 * pairs * tokens * columns * HEAD, bytes_accessed=8 * gathered.size,
            transcendentals=2 * pairs * tokens * columns,
        ),
        name="attention",
    )(own, lengths, plan, gathered, dout)
    return out, (near, far), carried


def run_own_half(own, gathered, dout, carried):
    tokens, width = dout.shape[1:]
    pairs = gathered.shape[0]
    columns = width // HEAD * tokens
    kv_shape = shape(pairs // 2, tokens, 2 * HEAD, dtype=BF16)
    query_grad, *kv_parts = pl.pallas_call(
        own_half_kernel,
        out_shape=(shape(tokens, width, dtype=BF16), kv_shape, kv_shape),
        in_specs=[SMEM] + [HBM] * 8,
        out_specs=[VMEM] * 3,
        scratch_shapes=[
            wide(1, pairs, tokens, 2 * HEAD, dtype=BF16), wide(tokens, width, dtype=BF16),
            wide(8, columns), wide(8, columns, dtype=jnp.int32),
            wide(columns, HEAD, dtype=BF16), wide(HEAD, columns, dtype=BF16),
            wide(HEAD, columns, dtype=BF16), wide(HEAD, columns),
            pltpu.SemaphoreType.DMA((9,)),
        ],
        compiler_params=PARAMS,
        cost_estimate=pl.CostEstimate(
            flops=8 * pairs * tokens * columns * HEAD, bytes_accessed=4 * gathered.size,
            transcendentals=pairs * tokens * columns,
        ),
        name="attention_own_half",
    )(own, gathered, dout, *carried)
    return query_grad, kv_parts


def on_device(
    x_in, dt_in, b_in, c_in, dy_in, a_log, d_skip, dt_bias,
    q_in, k_in, value_input, dout_in, doc_lengths, plan,
):
    seq_count = lax.axis_size("seq")
    own = lax.axis_index("seq").astype(jnp.int32).reshape(1)
    tokens = x_in.shape[1]
    mixer_inputs = (
        own, doc_lengths, x_in, dt_in, dy_in, b_in, c_in, a_log, dt_bias[None],
    )

    mixed = jnp.concatenate([q_in[0], k_in[0], value_input[0]], axis=1)
    gathered = lax.all_gather(mixed, "seq", axis=0, tiled=True)

    summary, *local = run_summary(*mixer_inputs)
    summaries = lax.all_gather(summary, "seq", axis=0)
    output, x_grad, dt_grad, bc_part, params = run_mixer(
        *mixer_inputs, d_skip[None], summaries, local
    )
    one_side = [(i, i ^ 1) for i in range(seq_count)]
    other_side = [(i, (((i + 1) ^ 1) - 1) % seq_count) for i in range(seq_count)]
    same_parity = [
        [*range(k, seq_count, 4), *range(k + 2, seq_count, 4)] for k in range(2)
    ]
    params = params + lax.ppermute(params, "seq", one_side)
    params = jnp.sum(lax.all_gather(params, "dp", axis=0), axis=0)
    rows = params.shape[0] // 2
    first = lax.rem(own[0], 4) < 2
    theirs = lax.ppermute(
        jnp.where(first, params[rows:], params[:rows]),
        "seq", [(i, i ^ 2) for i in range(seq_count)],
    )
    params = jnp.where(first, params[:rows], params[rows:]) + theirs
    split = jnp.concatenate([params[:, : 2 * HEAD], params[:, 2 * HEAD :]], 0).astype(BF16)
    split = jnp.pad(split, ((0, -2 * rows % 8), (0, 0)))
    gathered, split = lax.optimization_barrier((gathered, split))

    gathered = gathered.reshape(seq_count // 2, 2, tokens, -1)
    attn_out, kv_other, carried = run_attention(own, doc_lengths, plan, gathered, dout_in)
    arrived = [
        lax.ppermute(part, "seq", pairs) for part, pairs in zip(kv_other, (one_side, other_side))
    ]
    query_gradient, kv_own = run_own_half(own, gathered, dout_in, carried)
    kv_pair = [(a.astype(F32) + b.astype(F32)).astype(BF16) for a, b in zip(kv_own, arrived)]
    split = jnp.broadcast_to(split[None], (seq_count // 2, *split.shape))
    sent = jnp.concatenate([jnp.concatenate(kv_pair, 0), split], 1)
    sent, bc_part = lax.optimization_barrier((sent, bc_part))
    parts = lax.all_to_all(
        sent, "seq", split_axis=0, concat_axis=0, axis_index_groups=same_parity
    )
    bc_sum = jnp.sum(lax.all_gather(bc_part, "tp", axis=0), axis=0)
    kv_sum = jnp.sum(parts[:, :tokens].astype(F32), axis=0).astype(BF16)
    params_sum = parts[:, tokens : tokens + 2 * rows].astype(F32)
    params_sum = jnp.sum(params_sum.reshape(2, seq_count // 4, 2, rows, 2 * HEAD), axis=1)
    params_sum = jnp.concatenate([params_sum[:, 0], params_sum[:, 1]], 2).reshape(2 * rows, -1)
    return (
        output[None],
        x_grad[None],
        dt_grad[None],
        bc_sum[None, :NS],
        bc_sum[None, NS:],
        params_sum[:NS],
        params_sum[NS],
        params_sum[NS + 1],
        attn_out[None],
        query_gradient[None],
        kv_sum[None, :, :HEAD],
        kv_sum[None, :, HEAD:],
    )


def solution(mesh):
    tokens = P("dp", "seq", "tp")
    columns = P("dp", None, "seq")
    row = P("dp", None)
    return jax.shard_map(
        on_device,
        mesh=mesh,
        in_specs=(
            tokens, tokens, columns, columns, tokens, P(None, "tp"), P("tp"), P("tp"),
            tokens, tokens, tokens, tokens, row, row,
        ),
        out_specs=(
            tokens, tokens, tokens, columns, columns, P(None, "tp"), P("tp"), P("tp"),
            tokens, tokens, tokens, tokens,
        ),
        check_vma=False,
    )
```

```python
import jax
import jax.numpy as jnp
from jax import lax
from jax.experimental import pallas as pl
from jax.experimental.pallas import tpu as pltpu
from jax.sharding import PartitionSpec as P

NS = 16
HEAD = 128
BLOCK = 32
LANES = 128
SEGS = 8
RESET = 1e30
LOG2E = 1.4426950408889634
NEG = -1e30

F32 = jnp.float32
BF16 = jnp.bfloat16


def dot(a, b, dims=((1,), (0,)), precision=None):
    return lax.dot_general(a, b, (dims, ((), ())), precision=precision, preferred_element_type=F32)


def exact_dot(a, b, dims=((1,), (0,))):
    return dot(a, b, dims, lax.Precision.HIGHEST)


def iota(shape, axis):
    return lax.broadcasted_iota(jnp.int32, shape, axis)


def to_segments(tokens):
    span = tokens // SEGS
    row = iota((tokens, tokens), 0)
    token = iota((tokens, tokens), 1)
    return jnp.where(token == lax.rem(row, SEGS) * span + lax.div(row, SEGS), 1.0, 0.0)


def to_tokens(tokens):
    span = tokens // SEGS
    token = iota((tokens, tokens), 0)
    row = iota((tokens, tokens), 1)
    return jnp.where(row == lax.rem(token, span) * SEGS + lax.div(token, span), 1.0, 0.0)


def starts_of(lengths_ref):
    starts = [jnp.int32(0)]
    for k in range(lengths_ref.shape[1] - 1):
        starts.append(starts[-1] + lengths_ref[0, k])
    return starts


def begin_copies(pairs, semaphores):
    copies = [
        pltpu.make_async_copy(source, target, semaphores.at[k])
        for k, (source, target) in enumerate(pairs)
    ]
    for copy in copies:
        copy.start()
    return copies


def wait_all(copies):
    for copy in copies:
        copy.wait()


def softplus_of(raw):
    small = jnp.exp(-jnp.abs(raw))
    one = 1.0 + small
    tail = one - 1.0
    safe = jnp.where(tail == 0.0, 1.0, tail)
    log1p = jnp.where(tail == 0.0, small, jnp.log(one) * (small / safe))
    return jnp.maximum(raw, 0.0) + log1p


def with_resets(own_ref, lengths_ref, delta):
    tokens = delta.shape[0]
    span = tokens // SEGS
    row = iota(delta.shape, 0)
    token = own_ref[0] * tokens + lax.rem(row, SEGS) * span + lax.div(row, SEGS)
    first = token == 0
    for start in starts_of(lengths_ref):
        first = first | (token == start)
    return jnp.where(first, RESET, delta)


def spread(source, target):
    for n in range(NS):
        target[n] = jnp.broadcast_to(source[n : n + 1], target.shape[1:])


def fill_columns(segment, b_ref, c_ref, b_wide, c_wide):
    tokens = segment.shape[0]
    for source, target in ((b_ref, b_wide), (c_ref, c_wide)):
        columns = dot(segment, source[...], ((1,), (1,)))
        for n in range(NS):
            target[n] = jnp.broadcast_to(columns[:, n : n + 1], (tokens, LANES))


def shifted(value, by, fill):
    rows = value.shape[0]
    row = iota(value.shape, 0)
    moved = pltpu.roll(value, by % rows, 0)
    return jnp.where((row >= by) & (row < rows + by), moved, fill)


def summary_kernel(
    own_ref, lengths_hbm, x_hbm, dt_hbm, dy_hbm, b_hbm, c_hbm, a_hbm, bias_hbm,
    summary_ref, seg_state_ref, seg_adjoint_ref, seg_delta_ref,
    lengths_ref, x_ref, dt_ref, dy_ref, b_ref, c_ref, a_ref, bias_ref,
    rate2_ref, b_wide, c_wide, decay_delta, drive, upstream, before_ref, after_ref, rows_ref, semaphores,
):
    tokens, width = x_ref.shape
    span = tokens // SEGS
    copies = begin_copies(
        (
            (dt_hbm.at[0], dt_ref), (bias_hbm, bias_ref), (lengths_hbm, lengths_ref),
            (x_hbm.at[0], x_ref), (dy_hbm.at[0], dy_ref), (a_hbm, a_ref),
            (b_hbm.at[0], b_ref), (c_hbm.at[0], c_ref),
        ),
        semaphores,
    )
    segment = to_segments(tokens).astype(BF16)
    wait_all(copies[:3])
    raw = dot(segment, dt_ref[...]) + bias_ref[...]
    delta = softplus_of(raw)
    reset_delta = with_resets(own_ref, lengths_ref, delta)
    decay_delta[...] = reset_delta
    wait_all(copies[3:])
    drive[...] = delta * dot(segment, x_ref[...])
    upstream[...] = dot(segment, dy_ref[...])
    spread(-jnp.exp(a_ref[...]) * LOG2E, rate2_ref)
    fill_columns(segment, b_ref, c_ref, b_wide, c_wide)

    total = reset_delta[:SEGS]
    for pos in range(1, span):
        total = total + reset_delta[pos * SEGS : (pos + 1) * SEGS]
    seg_delta_ref[...] = total
    after = shifted(total, -1, 0.0)
    before = shifted(total, 1, 0.0)
    for by in (1, 2, 4):
        after = after + shifted(after, -by, 0.0)
        before = before + shifted(before, by, 0.0)
    after_ref[...] = after
    before_ref[...] = before
    whole = before[SEGS - 1 :] + total[SEGS - 1 :]
    high = whole.astype(BF16).astype(F32)
    low = whole - high
    ends = [part[:, lane : lane + LANES] for part in (high, low) for lane in range(0, width, LANES)]
    summary_ref[2 * NS * width // LANES :] = jnp.concatenate(ends, 0).astype(BF16)

    def state_row(n, carry):
        state_rows, adjoint_rows = [], []
        for lane in range(0, width, 4 * LANES):
            groups = [slice(k, k + LANES) for k in range(lane, lane + 4 * LANES, LANES)]
            rate2 = [rate2_ref[n, :, cols] for cols in groups]
            state = [jnp.zeros((SEGS, LANES), F32) for _ in groups]
            adjoint = list(state)
            decays = []
            for pos in range(span):
                rows = slice(pos * SEGS, (pos + 1) * SEGS)
                b_col = b_wide[n, rows]
                decays.append([])
                for k, cols in enumerate(groups):
                    decay = jnp.exp2(rate2[k] * decay_delta[rows, cols])
                    decays[pos].append(decay)
                    state[k] = decay * state[k] + b_col * drive[rows, cols]
            for pos in reversed(range(span)):
                rows = slice(pos * SEGS, (pos + 1) * SEGS)
                c_col = c_wide[n, rows]
                for k, cols in enumerate(groups):
                    adjoint[k] = decays[pos][k] * (c_col * upstream[rows, cols] + adjoint[k])
            for k, cols in enumerate(groups):
                seg_state_ref[n, :, cols] = state[k]
                seg_adjoint_ref[n, :, cols] = adjoint[k]
                weight = jnp.exp2(rate2[k] * after_ref[:, cols])
                state_rows.append(jnp.sum(weight * state[k], axis=0, keepdims=True))
                weight = jnp.exp2(rate2[k] * before_ref[:, cols])
                adjoint_rows.append(jnp.sum(weight * adjoint[k], axis=0, keepdims=True))
        rows_ref[n] = jnp.broadcast_to(jnp.concatenate(state_rows, 1), (SEGS, width))
        rows_ref[NS + n] = jnp.broadcast_to(jnp.concatenate(adjoint_rows, 1), (SEGS, width))
        return carry

    lax.fori_loop(0, NS, state_row, 0)
    gathered = jnp.concatenate([rows_ref[n, :1] for n in range(2 * NS)], 0)
    for k in range(width // LANES):
        rows = slice(2 * NS * k, 2 * NS * (k + 1))
        summary_ref[rows] = gathered[:, k * LANES : (k + 1) * LANES].astype(BF16)


def mixer_kernel(
    own_ref, lengths_hbm, x_hbm, dt_hbm, dy_hbm, b_hbm, c_hbm, a_hbm, bias_hbm, skip_hbm,
    summaries_hbm, seg_state_hbm, seg_adjoint_hbm, seg_delta_hbm,
    out_ref, x_grad_ref, dt_grad_ref, bc_ref, params_ref,
    lengths_ref, x_ref, dt_ref, dy_ref, b_ref, c_ref, a_ref, bias_ref, skip_ref,
    summaries_ref, seg_state_ref, seg_adjoint_ref, seg_delta_ref,
    rate_ref, enter_ref, arrive_ref, b_wide, c_wide,
    delta_ref, decay_delta, drive, upstream, y_acc, xg_acc, dd_acc, bg_acc, cg_acc, rate_acc,
    semaphores,
):
    tokens, width = x_ref.shape
    span = tokens // SEGS
    count = summaries_ref.shape[0]
    own = own_ref[0]
    copies = begin_copies(
        (
            (dt_hbm.at[0], dt_ref), (bias_hbm, bias_ref), (lengths_hbm, lengths_ref),
            (a_hbm, a_ref), (summaries_hbm, summaries_ref),
            (x_hbm.at[0], x_ref), (dy_hbm.at[0], dy_ref), (skip_hbm, skip_ref),
            (b_hbm.at[0], b_ref), (c_hbm.at[0], c_ref),
            (seg_state_hbm, seg_state_ref), (seg_adjoint_hbm, seg_adjoint_ref),
            (seg_delta_hbm, seg_delta_ref),
        ),
        semaphores,
    )
    segment = to_segments(tokens).astype(BF16)
    wait_all(copies[:3])
    delta = softplus_of(dot(segment, dt_ref[...]) + bias_ref[...])
    delta_ref[...] = delta
    decay_delta[...] = with_resets(own_ref, lengths_ref, delta)
    wait_all(copies[3:])
    drive[...] = delta * dot(segment, x_ref[...])
    upstream[...] = dot(segment, dy_ref[...])
    fill_columns(segment, b_ref, c_ref, b_wide, c_wide)
    rate_all = -jnp.exp(a_ref[...])
    rate2_all = rate_all * LOG2E
    spread(rate_all, rate_ref)

    entering = jnp.zeros((NS, width), F32)
    arriving = jnp.zeros((NS, width), F32)

    groups = width // LANES

    def factor(j):
        ends = summaries_ref[j, 2 * NS * groups :].astype(F32)
        ends = ends[:groups] + ends[groups:]
        return jnp.exp2(rate2_all * jnp.concatenate([ends[k : k + 1] for k in range(groups)], 1))

    def summed(j, first):
        starts = range(first, 2 * NS * groups, 2 * NS)
        return jnp.concatenate([summaries_ref[j, k : k + NS].astype(F32) for k in starts], 1)

    for j in range(count - 1):
        longer = factor(j) * entering + summed(j, 0)
        entering = jnp.where(j < own, longer, entering)
    for j in reversed(range(1, count)):
        longer = factor(j) * arriving + summed(j, NS)
        arriving = jnp.where(j > own, longer, arriving)
    spread(entering, enter_ref)
    spread(arriving, arrive_ref)

    y_acc[...] = jnp.zeros_like(y_acc)
    xg_acc[...] = jnp.zeros_like(xg_acc)
    dd_acc[...] = jnp.zeros_like(dd_acc)

    def state_row(n, carry):
        row = iota((SEGS, LANES), 0)
        for lane in range(0, width, 4 * LANES):
            groups = [slice(k, k + LANES) for k in range(lane, lane + 4 * LANES, LANES)]
            rate = [rate_ref[n, :, cols] for cols in groups]
            rate2 = [value * LOG2E for value in rate]
            state, adjoint = [], []
            for k, cols in enumerate(groups):
                seg_factor = jnp.exp2(rate2[k] * seg_delta_ref[:, cols])
                edge = enter_ref[n, :, cols]
                scale, total = seg_factor, seg_state_ref[n, :, cols]
                for by in (1, 2, 4):
                    total = total + scale * shifted(total, by, 0.0)
                    scale = scale * shifted(scale, by, 1.0)
                moved = pltpu.roll(total + scale * edge, 1, 0)
                state.append(jnp.where(row == 0, edge, moved))
                edge = arrive_ref[n, :, cols]
                scale, total = seg_factor, seg_adjoint_ref[n, :, cols]
                for by in (1, 2, 4):
                    total = total + scale * shifted(total, -by, 0.0)
                    scale = scale * shifted(scale, -by, 1.0)
                moved = pltpu.roll(total + scale * edge, SEGS - 1, 0)
                adjoint.append(jnp.where(row == SEGS - 1, edge, moved))
            decays, befores = [], []
            for pos in range(span):
                rows = slice(pos * SEGS, (pos + 1) * SEGS)
                b_col, c_col = b_wide[n, rows], c_wide[n, rows]
                decays.append([])
                befores.append(list(state))
                part = None
                for k, cols in enumerate(groups):
                    decay = jnp.exp2(rate2[k] * decay_delta[rows, cols])
                    decays[pos].append(decay)
                    state[k] = decay * state[k] + b_col * drive[rows, cols]
                    y_acc[rows, cols] += c_col * state[k]
                    term = upstream[rows, cols] * state[k]
                    part = term if part is None else part + term
                if lane == 0:
                    cg_acc[n, rows] = part
                else:
                    cg_acc[n, rows] += part
            rate_sum = [jnp.zeros((SEGS, LANES), F32) for _ in groups]
            for pos in reversed(range(span)):
                rows = slice(pos * SEGS, (pos + 1) * SEGS)
                b_col, c_col = b_wide[n, rows], c_wide[n, rows]
                part = None
                for k, cols in enumerate(groups):
                    full = c_col * upstream[rows, cols] + adjoint[k]
                    adjoint[k] = decays[pos][k] * full
                    xg_acc[rows, cols] += full * b_col
                    term = full * drive[rows, cols]
                    part = term if part is None else part + term
                    through = adjoint[k] * befores[pos][k]
                    dd_acc[rows, cols] += rate[k] * through
                    rate_sum[k] = rate_sum[k] + delta_ref[rows, cols] * through
                if lane == 0:
                    bg_acc[n, rows] = part
                else:
                    bg_acc[n, rows] += part
            for k, cols in enumerate(groups):
                rate_acc[n, :, cols] = rate[k] * rate_sum[k]
        return carry

    lax.fori_loop(0, NS, state_row, 0)

    token = to_tokens(tokens).astype(BF16)
    inputs = dot(segment, x_ref[...])
    skip = skip_ref[...]
    out_ref[...] = dot(token, (y_acc[...] + skip * inputs).astype(BF16)).astype(BF16)
    x_grad = xg_acc[...] * delta_ref[...] + skip * upstream[...]
    x_grad_ref[...] = dot(token, x_grad.astype(BF16)).astype(BF16)
    raw = dot(segment, dt_ref[...]) + bias_ref[...]
    raw_grad = (xg_acc[...] * inputs + dd_acc[...]) / (1.0 + jnp.exp(-raw))
    dt_grad_ref[...] = dot(token, raw_grad.astype(BF16)).astype(BF16)
    params_ref[:NS] = jnp.sum(rate_acc[...], axis=1)
    params_ref[NS : NS + 1] = jnp.sum(upstream[...] * inputs, axis=0, keepdims=True)
    params_ref[NS + 1 : NS + 2] = jnp.sum(raw_grad, axis=0, keepdims=True)
    lane = iota((tokens, LANES), 1)
    sums = jnp.zeros((tokens, LANES), F32)
    for k, source in enumerate((bg_acc, cg_acc)):
        for n in range(NS):
            total = jnp.sum(source[n], axis=1, keepdims=True)
            sums = jnp.where(lane == k * NS + n, total, sums)
    bc_ref[...] = exact_dot(sums.T[: 2 * NS], to_segments(tokens))


def by_head(ref):
    value = ref[...]
    return jnp.concatenate(
        [value[:, h : h + HEAD] for h in range(0, value.shape[1], HEAD)], 0
    )


def turn_back(ref, turned):
    tokens, width = ref.shape
    for h in range(width // HEAD):
        ref[:, h * HEAD : (h + 1) * HEAD] = (
            turned[:, h * tokens : (h + 1) * tokens].T.astype(ref.dtype)
        )


def key_value_copies(all_hbm, kv_ref, width):
    return [
        (all_hbm.at[:, k, :, width + v : width + v + HEAD], kv_ref.at[k, :, :, v : v + HEAD])
        for v in (0, HEAD)
        for k in range(2)
    ]


def keys_of(kv_ref, k):
    value = kv_ref[k, :, :, :HEAD]
    return value.reshape(-1, HEAD)


def values_of(kv_ref, k):
    value = kv_ref[k, :, :, HEAD:]
    return value.reshape(-1, HEAD)


def gradients(k, tokens, kv_ref, probs, query, d_att, dout_t, rowdot, kv_grad_refs):
    keys = keys_of(kv_ref, k)
    d_probs = dot(values_of(kv_ref, k), dout_t)
    d_scores = (probs * (d_probs - rowdot)).astype(BF16)
    key_grad = (dot(d_scores, query) * (HEAD ** -0.5)).astype(BF16)
    value_grad = dot(probs.astype(BF16), d_att).astype(BF16)
    for m in range(keys.shape[0] // tokens):
        rows = slice(m * tokens, (m + 1) * tokens)
        kv_grad_refs[m % 2][m // 2, :tokens, :HEAD] = key_grad[rows]
        kv_grad_refs[m % 2][m // 2, :tokens, HEAD:] = value_grad[rows]
    return dot(keys.astype(F32).T.astype(BF16), d_scores)


def inside(k, tokens, last, opening, dims):
    key = iota(dims, 0) * (2 * tokens) + iota(dims, 1) + k * tokens
    return ((key <= last) & (key >= opening)).reshape(dims[0] * dims[1], dims[2])


def attention_kernel(
    own_ref, lengths_ref, plan_ref, all_hbm, dout_hbm,
    out_ref, kv_near_ref, kv_far_ref, stats_ref, bounds_ref, query_ref, query_t, dout_t, query_acc,
    picked_ref, kv_ref, dout_ref, score_ref, semaphores,
):
    tokens, width = dout_ref.shape
    columns = width // HEAD * tokens
    places = tokens // BLOCK
    half = kv_ref.shape[1] * tokens
    factor = (HEAD ** -0.5) * LOG2E
    wanted = [plan_ref[0, own_ref[0] * places + p] for p in range(places)]
    picks = []
    for p, w in enumerate(wanted):
        device, place = lax.div(w, places), lax.rem(w, places)
        rows = pl.ds(pl.multiple_of(place * BLOCK, BLOCK), BLOCK)
        picks.append((
            all_hbm.at[lax.div(device, 2), lax.rem(device, 2), rows, :width],
            picked_ref.at[p * BLOCK : (p + 1) * BLOCK],
        ))
    picks = begin_copies(picks, semaphores.at[5:])
    rest = begin_copies(
        key_value_copies(all_hbm, kv_ref, width) + [(dout_hbm.at[0], dout_ref)], semaphores
    )

    column = lax.rem(iota((1, columns), 1), tokens)
    place = lax.div(column, BLOCK)
    block = jnp.zeros((1, columns), jnp.int32)
    for p, w in enumerate(wanted):
        block = jnp.where(place == p, w, block)
    last = block * BLOCK + lax.rem(column, BLOCK)
    opening = jnp.zeros((1, columns), jnp.int32)
    for start in starts_of(lengths_ref):
        opening = jnp.where(start <= last, start, opening)
    bounds_ref[:1] = last
    bounds_ref[1:2] = opening

    wait_all(picks)
    query = by_head(picked_ref)
    query_ref[...] = query
    query_t[...] = query.astype(F32).T.astype(BF16)
    wait_all(rest[:2])

    top = jnp.full((8, columns), NEG, F32)
    for k in range(2):
        scores = dot(keys_of(kv_ref, k), query_t[...])
        dims = (half // tokens, tokens, columns)
        scores = jnp.where(inside(k, tokens, last, opening, dims), scores, NEG)
        score_ref[k] = scores
        top = jnp.maximum(top, jnp.max(scores.reshape(half // 8, 8, columns), axis=0))
    shift = jnp.max(top, axis=0, keepdims=True) * factor

    wait_all(rest[2:])
    d_att = by_head(dout_ref)
    dout_t[...] = d_att.astype(F32).T.astype(BF16)
    total = jnp.zeros((8, columns), F32)
    attended = jnp.zeros((HEAD, columns), F32)
    other = 1 - lax.rem(own_ref[0], 2)
    for k in (1 - other, other):
        weights = jnp.exp2(score_ref[k] * factor - shift)
        value_t = values_of(kv_ref, k).astype(F32).T.astype(BF16)
        attended = attended + dot(value_t, weights.astype(BF16))
        total = total + jnp.sum(weights.reshape(half // 8, 8, columns), axis=0)
    total = jnp.sum(total, axis=0, keepdims=True)
    inverse = 1.0 / total
    attended = (attended * inverse).astype(BF16).astype(F32)
    turn_back(out_ref, attended)
    rowdot = jnp.sum(attended * dout_t[...].astype(F32), axis=0, keepdims=True)
    stats_ref[:1] = shift + jnp.log(total) * LOG2E
    stats_ref[1:2] = rowdot

    probs = weights * inverse
    query_acc[...] = gradients(
        other, tokens, kv_ref, probs, query, d_att, dout_t[...], rowdot,
        (kv_near_ref, kv_far_ref),
    )


def own_half_kernel(
    own_ref, all_hbm, dout_hbm, split_hbm, stats_hbm, bounds_hbm, query_hbm, query_t_hbm,
    dout_t_hbm, acc_hbm,
    query_grad_ref, sent_ref,
    kv_ref, dout_ref, split_ref, stats_ref, bounds_ref, query_ref, query_t, dout_t, query_acc,
    semaphores,
):
    count = sent_ref.shape[0]
    tokens, width = dout_ref.shape
    half = kv_ref.shape[1] * tokens
    columns = width // HEAD * tokens
    factor = (HEAD ** -0.5) * LOG2E
    own = lax.rem(own_ref[0], 2)
    copies = begin_copies(
        (
            (all_hbm.at[:, own, :, width : width + HEAD], kv_ref.at[0, :, :, :HEAD]),
            (query_t_hbm, query_t), (bounds_hbm, bounds_ref), (stats_hbm, stats_ref),
            (all_hbm.at[:, own, :, width + HEAD :], kv_ref.at[0, :, :, HEAD:]),
            (dout_t_hbm, dout_t), (query_hbm, query_ref), (dout_hbm.at[0], dout_ref),
            (acc_hbm, query_acc), (split_hbm, split_ref),
        ),
        semaphores,
    )
    wait_all(copies[:4])
    scores = dot(keys_of(kv_ref, 0), query_t[...])
    dims = (half // tokens, tokens, columns)
    valid = inside(own, tokens, bounds_ref[:1], bounds_ref[1:2], dims)
    probs = jnp.where(valid, jnp.exp2(scores * factor - stats_ref[:1]), 0.0)
    wait_all(copies[4:])
    for m in range(count):
        sent_ref[m, tokens:] = split_ref[...]
    part = gradients(
        0, tokens, kv_ref, probs, query_ref[...], by_head(dout_ref), dout_t[...],
        stats_ref[1:2], (sent_ref.at[: count // 2], sent_ref.at[count // 2 :]),
    )
    turn_back(query_grad_ref, (query_acc[...] + part) * (HEAD ** -0.5))


VMEM = pl.BlockSpec(memory_space=pltpu.VMEM)
SMEM = pl.BlockSpec(memory_space=pltpu.SMEM)
HBM = pl.BlockSpec(memory_space=pltpu.HBM)
PARAMS = pltpu.CompilerParams(vmem_limit_bytes=63 * 1024 * 1024)


def shape(*dims, dtype=F32):
    return jax.ShapeDtypeStruct(dims, dtype)


def wide(*dims, dtype=F32):
    return pltpu.VMEM(dims, dtype)


def run_summary(own, lengths, x, dt, dy, b, c, a_log, bias):
    tokens, width = x.shape[1:]
    return pl.pallas_call(
        summary_kernel,
        out_shape=(
            shape(2 * (NS + 1) * width // LANES, LANES, dtype=BF16),
            shape(NS, SEGS, width), shape(NS, SEGS, width), shape(SEGS, width),
        ),
        in_specs=[SMEM] + [HBM] * 8,
        out_specs=[VMEM] * 4,
        scratch_shapes=[
            pltpu.SMEM(lengths.shape, jnp.int32),
            wide(tokens, width, dtype=BF16), wide(tokens, width, dtype=BF16),
            wide(tokens, width, dtype=BF16),
            wide(NS, tokens, dtype=BF16), wide(NS, tokens, dtype=BF16),
            wide(NS, width), wide(1, width),
            wide(NS, SEGS, width), wide(NS, tokens, LANES), wide(NS, tokens, LANES),
            wide(tokens, width), wide(tokens, width), wide(tokens, width),
            wide(SEGS, width), wide(SEGS, width), wide(2 * NS, SEGS, width),
            pltpu.SemaphoreType.DMA((8,)),
        ],
        compiler_params=PARAMS,
        name="mixer_summary",
    )(own, lengths, x, dt, dy, b, c, a_log, bias)


def run_mixer(own, lengths, x, dt, dy, b, c, a_log, bias, skip, summaries, local):
    tokens, width = x.shape[1:]
    return pl.pallas_call(
        mixer_kernel,
        out_shape=(
            shape(tokens, width, dtype=BF16), shape(tokens, width, dtype=BF16),
            shape(tokens, width, dtype=BF16), shape(2 * NS, tokens), shape(NS + 2, width),
        ),
        in_specs=[SMEM] + [HBM] * 13,
        out_specs=[VMEM] * 5,
        scratch_shapes=[
            pltpu.SMEM(lengths.shape, jnp.int32),
            wide(tokens, width, dtype=BF16), wide(tokens, width, dtype=BF16),
            wide(tokens, width, dtype=BF16),
            wide(NS, tokens, dtype=BF16), wide(NS, tokens, dtype=BF16),
            wide(NS, width), wide(1, width), wide(1, width),
            wide(*summaries.shape, dtype=BF16),
            wide(NS, SEGS, width), wide(NS, SEGS, width), wide(SEGS, width),
            wide(NS, SEGS, width), wide(NS, SEGS, width), wide(NS, SEGS, width),
            wide(NS, tokens, LANES), wide(NS, tokens, LANES),
            wide(tokens, width), wide(tokens, width), wide(tokens, width), wide(tokens, width),
            wide(tokens, width), wide(tokens, width), wide(tokens, width),
            wide(NS, tokens, LANES), wide(NS, tokens, LANES),
            wide(NS, SEGS, width),
            pltpu.SemaphoreType.DMA((13,)),
        ],
        compiler_params=PARAMS,
        name="mixer",
    )(own, lengths, x, dt, dy, b, c, a_log, bias, skip, summaries, *local)


def run_attention(own, lengths, plan, gathered, dout):
    tokens, width = dout.shape[1:]
    pairs = gathered.shape[0]
    columns = width // HEAD * tokens
    kv_shape = shape(pairs // 2, tokens, 2 * HEAD, dtype=BF16)
    out, near, far, *carried = pl.pallas_call(
        attention_kernel,
        out_shape=(
            shape(tokens, width, dtype=BF16), kv_shape, kv_shape,
            shape(8, columns), shape(8, columns, dtype=jnp.int32),
            shape(columns, HEAD, dtype=BF16), shape(HEAD, columns, dtype=BF16),
            shape(HEAD, columns, dtype=BF16), shape(HEAD, columns),
        ),
        in_specs=[SMEM] * 3 + [HBM] * 2,
        out_specs=[VMEM] * 9,
        scratch_shapes=[
            wide(tokens, width, dtype=BF16), wide(2, pairs, tokens, 2 * HEAD, dtype=BF16),
            wide(tokens, width, dtype=BF16), wide(2, pairs * tokens, columns),
            pltpu.SemaphoreType.DMA((5 + tokens // BLOCK,)),
        ],
        compiler_params=PARAMS,
        cost_estimate=pl.CostEstimate(
            flops=10 * pairs * tokens * columns * HEAD, bytes_accessed=8 * gathered.size,
            transcendentals=2 * pairs * tokens * columns,
        ),
        name="attention",
    )(own, lengths, plan, gathered, dout)
    return out, (near, far), carried


def run_own_half(own, gathered, dout, split, carried):
    tokens, width = dout.shape[1:]
    pairs = gathered.shape[0]
    columns = width // HEAD * tokens
    return pl.pallas_call(
        own_half_kernel,
        out_shape=(
            shape(tokens, width, dtype=BF16),
            shape(pairs, tokens + split.shape[0], 2 * HEAD, dtype=BF16),
        ),
        in_specs=[SMEM] + [HBM] * 9,
        out_specs=[VMEM] * 2,
        scratch_shapes=[
            wide(1, pairs, tokens, 2 * HEAD, dtype=BF16), wide(tokens, width, dtype=BF16),
            wide(*split.shape, dtype=BF16),
            wide(8, columns), wide(8, columns, dtype=jnp.int32),
            wide(columns, HEAD, dtype=BF16), wide(HEAD, columns, dtype=BF16),
            wide(HEAD, columns, dtype=BF16), wide(HEAD, columns),
            pltpu.SemaphoreType.DMA((10,)),
        ],
        compiler_params=PARAMS,
        name="attention_own_half",
    )(own, gathered, dout, split, *carried)


def on_device(
    x_in, dt_in, b_in, c_in, dy_in, a_log, d_skip, dt_bias,
    q_in, k_in, value_input, dout_in, doc_lengths, plan,
):
    seq_count = lax.axis_size("seq")
    own = lax.axis_index("seq").astype(jnp.int32).reshape(1)
    tokens = x_in.shape[1]
    mixer_inputs = (
        own, doc_lengths, x_in, dt_in, dy_in, b_in, c_in, a_log, dt_bias[None],
    )

    mixed = jnp.concatenate([q_in[0], k_in[0], value_input[0]], axis=1)
    gathered = lax.all_gather(mixed, "seq", axis=0, tiled=True)

    summary, *local = run_summary(*mixer_inputs)
    summaries = lax.all_gather(summary, "seq", axis=0)
    output, x_grad, dt_grad, bc_part, params = run_mixer(
        *mixer_inputs, d_skip[None], summaries, local
    )
    one_side = [(i, i ^ 1) for i in range(seq_count)]
    other_side = [(i, (((i + 1) ^ 1) - 1) % seq_count) for i in range(seq_count)]
    same_parity = [
        [*range(k, seq_count, 4), *range(k + 2, seq_count, 4)] for k in range(2)
    ]
    params = params + lax.ppermute(params, "seq", one_side)
    params = jnp.sum(lax.all_gather(params, "dp", axis=0), axis=0)
    rows = params.shape[0] // 2
    first = lax.rem(own[0], 4) < 2
    theirs = lax.ppermute(
        jnp.where(first, params[rows:], params[:rows]),
        "seq", [(i, i ^ 2) for i in range(seq_count)],
    )
    params = jnp.where(first, params[:rows], params[rows:]) + theirs
    split = jnp.concatenate([params[:, : 2 * HEAD], params[:, 2 * HEAD :]], 0).astype(BF16)
    split = jnp.pad(split, ((0, -2 * rows % 8), (0, 0)))
    gathered, split = lax.optimization_barrier((gathered, split))

    gathered = gathered.reshape(seq_count // 2, 2, tokens, -1)
    attn_out, kv_other, carried = run_attention(own, doc_lengths, plan, gathered, dout_in)
    arrived = [
        lax.ppermute(part, "seq", pairs) for part, pairs in zip(kv_other, (one_side, other_side))
    ]
    query_gradient, sent = run_own_half(own, gathered, dout_in, split, carried)
    arrived = jnp.pad(jnp.concatenate(arrived, 0), ((0, 0), (0, split.shape[0]), (0, 0)))
    sent = (sent.astype(F32) + arrived.astype(F32)).astype(BF16)
    sent, bc_part = lax.optimization_barrier((sent, bc_part))
    parts = lax.all_to_all(
        sent, "seq", split_axis=0, concat_axis=0, axis_index_groups=same_parity
    )
    bc_sum = jnp.sum(lax.all_gather(bc_part, "tp", axis=0), axis=0)
    kv_sum = jnp.sum(parts[:, :tokens].astype(F32), axis=0).astype(BF16)
    params_sum = parts[:, tokens : tokens + 2 * rows].astype(F32)
    params_sum = jnp.sum(params_sum.reshape(2, seq_count // 4, 2, rows, 2 * HEAD), axis=1)
    params_sum = jnp.concatenate([params_sum[:, 0], params_sum[:, 1]], 2).reshape(2 * rows, -1)
    return (
        output[None],
        x_grad[None],
        dt_grad[None],
        bc_sum[None, :NS],
        bc_sum[None, NS:],
        params_sum[:NS],
        params_sum[NS],
        params_sum[NS + 1],
        attn_out[None],
        query_gradient[None],
        kv_sum[None, :, :HEAD],
        kv_sum[None, :, HEAD:],
    )


def solution(mesh):
    tokens = P("dp", "seq", "tp")
    columns = P("dp", None, "seq")
    row = P("dp", None)
    return jax.shard_map(
        on_device,
        mesh=mesh,
        in_specs=(
            tokens, tokens, columns, columns, tokens, P(None, "tp"), P("tp"), P("tp"),
            tokens, tokens, tokens, tokens, row, row,
        ),
        out_specs=(
            tokens, tokens, tokens, columns, columns, P(None, "tp"), P("tp"), P("tp"),
            tokens, tokens, tokens, tokens,
        ),
        check_vma=False,
    )
```
